32 devices in a mesh: tile: 8 (over z, y), cuts: 4 (over x, core).
Axes of the slice: x: 2, y: 2, z: 4, core: 2. Of those that a mesh axis runs over, the one named last changes fastest.
Arguments:
- transmission: float32 [4, 2, 2048, 1024], P('cuts', None, 'tile')
- probe: float32 [2, 256, 256], replicated, may hold values from -6 to 6
- prop_phase: float32 [256, 256], replicated, may hold values from -3.140625 to 3.140625
- row_off: int32 [8], P('tile'), may hold values from 0 to 255
- col_off: int32 [8], P('tile'), may hold values from 0 to 768
- measured: float32 [8, 256, 256], P('tile'), may hold values from 0 to 1.6
Outputs:
- obj_grad: float32 [4, 2, 2048, 1024], P('cuts', None, 'tile')
The draws below stay inside these ranges and needn't reach their ends.
All inputs are finite; a program needn't handle non-finite values.
Results may differ from the reference program's by a relative error of at most 0.0003.
Values sent between devices are 32-bit elements; how exact they have to be, the bound alone decides.
No kernel may reach another device: no remote copies, remote signals or barrier semaphores. Data moves between devices by JAX's collectives and lax.ppermute only.
A program may use at most 64 MiB of HBM per device.

```python
import jax
import jax.numpy as jnp
from jax import lax

WIN = 256
OBJ_COLS = 1024
STRIP_ROWS = 256
POS_DEV = 1
SLICES = 4
OBJ_ROWS = 2048
POSITIONS = 8


def draw_transmission(key, part):
    shape = (SLICES, 2, OBJ_ROWS, OBJ_COLS)
    noise = 0.2 * jax.random.normal(key, shape, jnp.float32)
    offset = jnp.array([0.95, 0.0], jnp.float32).reshape(1, 2, 1, 1)
    return offset + noise


def set_ends(drawn, key, smallest, largest):
    place = [jax.random.randint(jax.random.fold_in(key, axis), (), 0, length) for axis, length in enumerate(drawn.shape)]
    main_axis = drawn.shape.index(max(drawn.shape))
    neighbour = place[:main_axis] + [(place[main_axis] + 1) % drawn.shape[main_axis]] + place[main_axis + 1:]
    return drawn.at[tuple(place)].set(smallest).at[tuple(neighbour)].set(largest)


def levels(rng, shape, cuts, low, largest):
    factor_of, own = 1.0, jax.random.fold_in(rng, 6)
    for axis_at, blocks in cuts:
        heights = jnp.exp(jax.random.uniform(jax.random.fold_in(own, axis_at), (blocks,), jnp.float32, low / len(cuts), largest / len(cuts)))
        factor_of = factor_of * jnp.repeat(heights, shape[axis_at] // blocks).reshape([-1 if axis == axis_at else 1 for axis in range(len(shape))])
    return factor_of


def centred(rng, extent, scale, limit, kind=jnp.bfloat16):
    return jnp.clip(scale * jax.random.normal(rng, extent, jnp.float32), -limit, limit).astype(kind)


def setup_inputs(seed: int = 0) -> dict:
    key_of = jax.random.split(jax.random.key(seed), 7)
    transmission = draw_transmission(jax.random.fold_in(key_of[6], 71), 0)
    probe = centred(key_of[1], (2, WIN, WIN), 0.7071, 6.0, jnp.float32)
    prop_phase = jnp.clip(jax.random.uniform(key_of[2], (WIN, WIN), jnp.float32, -3.140625, 3.140625), -3.140625, 3.140625)
    row_off = set_ends(jax.random.randint(key_of[3], (POSITIONS,), 0, STRIP_ROWS), jax.random.fold_in(key_of[3], 1), 0, STRIP_ROWS - 1).astype(jnp.int32)
    col_off = set_ends(jax.random.randint(key_of[4], (POSITIONS,), 0, OBJ_COLS - WIN + 1), jax.random.fold_in(key_of[4], 1), 0, OBJ_COLS - WIN).astype(jnp.int32)
    measured = jnp.clip(1.6 * jax.random.uniform(key_of[5], (POSITIONS, WIN, WIN), jnp.float32) ** levels(key_of[5], (POSITIONS, WIN, WIN), ((0, 8),), -0.2, 0.2), 0.0, 1.6)
    return {"transmission": transmission, "probe": probe, "prop_phase": prop_phase, "row_off": row_off, "col_off": col_off, "measured": measured}


def forward_fft(field):
    return jnp.fft.fft2(field, norm="ortho")


def inverse_fft(field):
    return jnp.fft.ifft2(field, norm="ortho")


def reference(transmission, probe, prop_phase, row_off, col_off, measured):
    total_rows = transmission.shape[2]
    padded = jnp.pad(transmission, ((0, 0), (0, 0), (0, WIN), (0, 0)))
    kernel = jnp.exp(1j * prop_phase)
    probe_wave = probe[0] + 1j * probe[1]
    strips = jnp.arange(POSITIONS, dtype=jnp.int32) // POS_DEV
    top_rows = (strips * STRIP_ROWS + row_off).astype(jnp.int32)
    zero = jnp.zeros((), jnp.int32)

    def accumulate(gradient, inputs):
        row, column, intensity = inputs
        start = (zero, zero, row, column)
        patch = lax.dynamic_slice(padded, start, (SLICES, 2, WIN, WIN))
        layers_complex = patch[:, 0] + 1j * patch[:, 1]
        wave = probe_wave
        saved = []
        for layer in range(SLICES):
            saved.append(wave)
            wave = inverse_fft(kernel * forward_fft(wave * layers_complex[layer]))
        far = forward_fft(wave)
        residual = jnp.real(far) ** 2 + jnp.imag(far) ** 2 - intensity
        back = inverse_fft(residual * far)
        pieces = [None] * SLICES
        for layer in range(SLICES - 1, -1, -1):
            inner = inverse_fft(jnp.conj(kernel) * forward_fft(back))
            pieces[layer] = jnp.conj(saved[layer]) * inner
            back = jnp.conj(layers_complex[layer]) * inner
        stacked = jnp.stack(pieces, axis=0)
        piece = jnp.stack([jnp.real(stacked), jnp.imag(stacked)], axis=1)
        current = lax.dynamic_slice(gradient, start, piece.shape)
        gradient = lax.dynamic_update_slice(gradient, current + piece.astype(gradient.dtype), start)
        return gradient, None

    initial = jnp.zeros(padded.shape, jnp.float32)
    gradient, _ = lax.scan(accumulate, initial, (top_rows, col_off, measured))
    return gradient[:, :, :total_rows]
```

```python
import jax
import jax.numpy as jnp
import ml_dtypes
import numpy as np
from jax import lax
from jax.experimental import pallas as pl
from jax.experimental.pallas import tpu as pltpu
from jax.sharding import PartitionSpec as P

f32, bf16 = jnp.float32, jnp.bfloat16
LANE = 128
VMEM = pl.BlockSpec(memory_space=pltpu.VMEM)
SMEM = pl.BlockSpec(memory_space=pltpu.SMEM)
ANY = pl.BlockSpec(memory_space=pl.ANY)
PARAMS = pltpu.CompilerParams(vmem_limit_bytes=48 << 20)


def dft_tables(n):
    half = n // 2
    k = np.arange(half)[:, None]
    m = np.arange(half)[None, :]

    def real_form(odd):
        angle = -2 * np.pi * ((k * (2 * m + odd)) % n) / n
        c, s = np.cos(angle) / np.sqrt(n), np.sin(angle) / np.sqrt(n)
        return np.block([[c, s], [-s, c]])

    def parts(matrix, axis):
        high = matrix.astype(np.float32).astype(ml_dtypes.bfloat16)
        low = (matrix - high.astype(np.float64)).astype(np.float32).astype(ml_dtypes.bfloat16)
        return np.concatenate([high, high, low], axis=axis)

    even, odd = real_form(0), real_form(1)
    right_fwd = np.stack([parts(even, 0), parts(odd, 0)])
    left_fwd = np.stack([parts(even.T, 1), parts(odd.T, 1)])
    left_inv = np.stack([parts(even, 1), parts(odd, 1)])
    right_inv = np.stack([parts(even.T, 0), parts(odd.T, 0)])
    return right_fwd, left_fwd, left_inv, right_inv


def split(x, axis):
    high = x.astype(bf16)
    low = (x - high.astype(f32)).astype(bf16)
    return jnp.concatenate([high, low, high], axis=axis)


def right_dot(x, table):
    return jnp.dot(split(x, 1), table, preferred_element_type=f32)


def left_dot(table, x):
    return jnp.dot(table, split(x, 0), preferred_element_type=f32)


def to_rows(a, b):
    h = a.shape[0] // 2

    def one(r):
        re = jnp.concatenate([a[r : r + h, :h], b[r : r + h, :h]], 1)
        im = jnp.concatenate([a[r : r + h, h:], b[r : r + h, h:]], 1)
        return jnp.concatenate([re, im], 0)

    return one(0), one(h)


def to_columns(a, b):
    h = a.shape[0] // 2

    def one(c):
        top = jnp.concatenate([a[:h, c : c + h], a[h:, c : c + h]], 1)
        bottom = jnp.concatenate([b[:h, c : c + h], b[h:, c : c + h]], 1)
        return jnp.concatenate([top, bottom], 0)

    return one(0), one(h)


def columns_of(re, im):
    h = re.shape[1] // 2
    return (
        jnp.concatenate([re[:, :h], im[:, :h]], 1),
        jnp.concatenate([re[:, h:], im[:, h:]], 1),
    )


def planes_of(a, b):
    h = a.shape[1] // 2
    return (
        jnp.concatenate([a[:, :h], b[:, :h]], 1),
        jnp.concatenate([a[:, h:], b[:, h:]], 1),
    )


def forward(re, im, right, left):
    a, b = columns_of(re, im)
    a, b = to_rows(right_dot(a + b, right[0]), right_dot(a - b, right[1]))
    return left_dot(left[0], a + b), left_dot(left[1], a - b)


def inverse(a, b, left, right):
    p, q = left_dot(left[0], a), left_dot(left[1], b)
    a, b = to_columns(p + q, p - q)
    p, q = right_dot(a, right[0]), right_dot(b, right[1])
    return planes_of(p + q, p - q)


def times(ar, ai, br, bi):
    return ar * br - ai * bi, ar * bi + ai * br


def conj_times(ar, ai, br, bi):
    return ar * br + ai * bi, ar * bi - ai * br


def by_phase(a, b, cosine, sine):
    h = a.shape[0] // 2
    out = []
    for i, x in enumerate((a, b)):
        at = slice(i * h, (i + 1) * h)
        re, im = times(x[:h], x[h:], cosine[at], sine[at])
        out.append(jnp.concatenate([re, im], 0))
    return out


def by_residual(a, b, observed):
    h = a.shape[0] // 2
    out = []
    for i, x in enumerate((a, b)):
        re, im = x[:h], x[h:]
        residual = re * re + im * im - observed[i * h : (i + 1) * h]
        out.append(jnp.concatenate([residual * re, residual * im], 0))
    return out


def chain(cut, patches, probe, cosine, sine, observed, tables):
    n = probe.shape[1]
    sections = len(patches)

    def kernel(cut_ref, *refs):
        sources = refs[:sections]
        probe, cosine, sine, observed, rf, lf, li, ri, out, patch, waves, sems = refs[sections:]
        me = cut_ref[0]

        def fetch(i):
            to = me ^ i
            return pltpu.make_async_copy(sources[i], patch.at[to], sems.at[to])

        for i in range(sections):
            fetch(i).start()

        def wave(s):
            return (probe[0], probe[1]) if s == 0 else (waves[s - 1, 0], waves[s - 1, 1])

        for s in range(sections):
            pltpu.make_async_copy(sources[0], patch.at[s], sems.at[s]).wait()
            re, im = times(*wave(s), patch[s, 0], patch[s, 1])
            a, b = forward(re, im, rf, lf)
            if s < sections - 1:
                a, b = by_phase(a, b, cosine[...], sine[...])
                re, im = inverse(a, b, li, ri)
                waves[s, 0] = re
                waves[s, 1] = im
        a, b = by_residual(a, b, observed)
        re, im = inverse(a, b, li, ri)
        for s in range(sections - 1, -1, -1):

            @pl.when(me == s)
            def _(s=s, re=re, im=im):
                out[0], out[1] = conj_times(*wave(s), re, im)

            if s > 0:
                re, im = conj_times(patch[s, 0], patch[s, 1], re, im)
                a, b = forward(re, im, rf, lf)
                a, b = by_phase(a, b, cosine[...], -sine[...])
                re, im = inverse(a, b, li, ri)

    return pl.pallas_call(
        kernel,
        out_shape=jax.ShapeDtypeStruct((2, n, n), f32),
        in_specs=[SMEM] + [ANY] * sections + [VMEM] * 8,
        out_specs=VMEM,
        scratch_shapes=[
            pltpu.VMEM((sections, 2, n, n), f32),
            pltpu.VMEM((sections - 1, 2, n, n), f32),
            pltpu.SemaphoreType.DMA((sections,)),
        ],
        compiler_params=PARAMS,
    )(cut, *patches, probe, cosine, sine, observed, *tables)


def window_start(column, width, columns):
    start = jnp.minimum(column // LANE * LANE, columns - width - LANE)
    return pl.multiple_of(start, LANE), column - start


def cut_window(offsets, strip, width):
    _, _, rows, columns = strip.shape

    def kernel(offsets, strip, out, wide, sem):
        row, column = offsets[0], offsets[1]
        start, shift = window_start(column, width, columns)
        copy = pltpu.make_async_copy(strip.at[0, :, :, pl.ds(start, width + LANE)], wide, sem)
        copy.start()
        copy.wait()
        for c in range(2):
            x = pltpu.roll(wide[c], lax.rem(width + LANE - shift, width + LANE), 1)[:, :width]
            out[c] = pltpu.roll(x, lax.rem(rows - row, rows), 0)

    return pl.pallas_call(
        kernel,
        out_shape=jax.ShapeDtypeStruct((2, rows, width), f32),
        in_specs=[SMEM, ANY],
        out_specs=VMEM,
        scratch_shapes=[pltpu.VMEM((2, rows, width + LANE), f32), pltpu.SemaphoreType.DMA],
        compiler_params=PARAMS,
    )(offsets, strip)


def place(own_offsets, came_offsets, own, came, columns):
    _, rows, width = own.shape

    def kernel(own_offsets, came_offsets, own, came, out):
        index = lax.broadcasted_iota(jnp.int32, (rows, width), 0)
        out[...] = jnp.zeros_like(out)
        for offsets, piece, is_own in ((own_offsets, own, True), (came_offsets, came, False)):
            row, column = offsets[0], offsets[1]
            start, shift = window_start(column, width, columns)
            keep = index >= row if is_own else index < row
            for c in range(2):
                x = jnp.where(keep, pltpu.roll(piece[c], row, 0), 0.0)
                x = jnp.concatenate([x, jnp.zeros((rows, LANE), f32)], 1)
                at = (0, c, slice(None), pl.ds(start, width + LANE))
                out[at] = out[at] + pltpu.roll(x, shift, 1)

    return pl.pallas_call(
        kernel,
        out_shape=jax.ShapeDtypeStruct((1, 2, rows, columns), f32),
        in_specs=[SMEM, SMEM, VMEM, VMEM],
        out_specs=VMEM,
        compiler_params=PARAMS,
    )(own_offsets, came_offsets, own, came)


def shifted(value, by):
    devices = lax.axis_size("tile")
    pairs = [(i, i + by) for i in range(devices) if 0 <= i + by < devices]
    return lax.ppermute(value, "tile", pairs)


def swapped(value, bit):
    devices = lax.axis_size("cuts")
    return lax.ppermute(value, "cuts", [(i, i ^ bit) for i in range(devices)])


def by_parity(x):
    n = x.shape[-1]
    return x.reshape(n // 2, 2, n // 2, 2).transpose(1, 0, 3, 2).reshape(n, n)


def per_device(transmission, probe, prop_phase, row_off, col_off, measured):
    columns = transmission.shape[3]
    width = probe.shape[1]
    offsets = jnp.concatenate([row_off, col_off])
    came_offsets = shifted(offsets, 1)
    own = cut_window(offsets, transmission, width)
    tables = [jnp.asarray(t) for t in dft_tables(width)]
    phase = by_parity(prop_phase)
    cosine, sine = jnp.cos(phase), jnp.sin(phase)
    observed = by_parity(measured[0])
    band = shifted(cut_window(came_offsets, transmission, width), -1)
    index = lax.broadcasted_iota(jnp.int32, own.shape, 1)
    patch = jnp.where(index < own.shape[1] - row_off[0], own, band)
    across = swapped(patch, 2)
    patches = [patch, swapped(patch, 1), across, swapped(across, 1)]
    cut = lax.axis_index("cuts").astype(jnp.int32).reshape(1)
    piece = chain(cut, patches, probe, cosine, sine, observed, tables)
    came = shifted(piece, 1)
    return place(offsets, came_offsets, piece, came, columns)


def solution(mesh):
    placed = (P("cuts", None, "tile", None), P(), P(), P("tile"), P("tile"), P("tile", None, None))
    return jax.shard_map(
        per_device,
        mesh=mesh,
        in_specs=placed,
        out_specs=P("cuts", None, "tile", None),
        check_vma=False,
    )
```

```python
import jax
import jax.numpy as jnp
import numpy as np
from jax import lax
from jax.experimental import pallas as pl
from jax.experimental.pallas import tpu as pltpu
from jax.sharding import PartitionSpec as P

f32, bf16 = jnp.float32, jnp.bfloat16
LANE = 128
VMEM = pl.BlockSpec(memory_space=pltpu.VMEM)
SMEM = pl.BlockSpec(memory_space=pltpu.SMEM)
ANY = pl.BlockSpec(memory_space=pl.ANY)
HBM = pl.BlockSpec(memory_space=pltpu.HBM)
SHORT = pl.CostEstimate(flops=1 << 16, bytes_accessed=1 << 12, transcendentals=0)
PARAMS = pltpu.CompilerParams(vmem_limit_bytes=12 << 20)


def dft_tables(n):
    half = n // 2
    k = np.arange(half)[:, None]
    m = np.arange(half)[None, :]

    def real_form(odd):
        angle = -2 * np.pi * ((k * (2 * m + odd)) % n) / n
        c, s = np.cos(angle) / np.sqrt(n), np.sin(angle) / np.sqrt(n)
        return np.block([[c, s], [-s, c]])

    def parts(matrix, axis):
        high = matrix.astype(np.float32).astype(jnp.bfloat16)
        low = (matrix - high.astype(np.float64)).astype(np.float32).astype(jnp.bfloat16)
        return np.concatenate([high, high, low], axis=axis)

    even, odd = real_form(0), real_form(1)
    right = np.stack([parts(m, 0) for m in (even, odd, even.T, odd.T)])
    left = np.stack([parts(m, 1) for m in (even.T, odd.T, even, odd)])
    return right, left


def pinned(x):
    return pltpu.with_memory_space_constraint(x, pltpu.HBM)


def split(x, axis):
    high = x.astype(bf16)
    low = (x - high.astype(f32)).astype(bf16)
    return jnp.concatenate([high, low, high], axis=axis)


def right_dot(x, table):
    return jnp.dot(split(x, 1), table, preferred_element_type=f32)


def left_dot(table, x):
    return jnp.dot(table, split(x, 0), preferred_element_type=f32)


def to_rows(a, b):
    h = a.shape[0] // 2

    def one(r):
        re = jnp.concatenate([a[r : r + h, :h], b[r : r + h, :h]], 1)
        im = jnp.concatenate([a[r : r + h, h:], b[r : r + h, h:]], 1)
        return jnp.concatenate([re, im], 0)

    return one(0), one(h)


def to_columns(a, b):
    h = a.shape[0] // 2

    def one(c):
        top = jnp.concatenate([a[:h, c : c + h], a[h:, c : c + h]], 1)
        bottom = jnp.concatenate([b[:h, c : c + h], b[h:, c : c + h]], 1)
        return jnp.concatenate([top, bottom], 0)

    return one(0), one(h)


def columns_of(re, im):
    h = re.shape[1] // 2
    return (
        jnp.concatenate([re[:, :h], im[:, :h]], 1),
        jnp.concatenate([re[:, h:], im[:, h:]], 1),
    )


def planes_of(a, b):
    h = a.shape[1] // 2
    return (
        jnp.concatenate([a[:, :h], b[:, :h]], 1),
        jnp.concatenate([a[:, h:], b[:, h:]], 1),
    )


def forward(re, im, tables):
    right, left = tables
    a, b = columns_of(re, im)
    a, b = to_rows(right_dot(a + b, right[0]), right_dot(a - b, right[1]))
    return left_dot(left[0], a + b), left_dot(left[1], a - b)


def inverse(a, b, tables):
    right, left = tables
    p, q = left_dot(left[2], a), left_dot(left[3], b)
    a, b = to_columns(p + q, p - q)
    p, q = right_dot(a, right[2]), right_dot(b, right[3])
    return planes_of(p + q, p - q)


def times(ar, ai, br, bi):
    return ar * br - ai * bi, ar * bi + ai * br


def conj_times(ar, ai, br, bi):
    return ar * br + ai * bi, ar * bi - ai * br


def by_phase(a, b, cosine, sine):
    h = a.shape[0] // 2
    out = []
    for i, x in enumerate((a, b)):
        at = slice(i * h, (i + 1) * h)
        re, im = times(x[:h], x[h:], cosine[at], sine[at])
        out.append(jnp.concatenate([re, im], 0))
    return out


def by_residual(a, b, observed):
    h = a.shape[0] // 2
    out = []
    for i, x in enumerate((a, b)):
        re, im = x[:h], x[h:]
        residual = re * re + im * im - observed[i * h : (i + 1) * h]
        out.append(jnp.concatenate([residual * re, residual * im], 0))
    return out


def prepare(prop_phase, *patterns):
    n = prop_phase.shape[0]

    def kernel(phase, *refs):
        observed, outs, (held, sem) = refs[: len(patterns)], refs[len(patterns) : -2], refs[-2:]
        row = lax.broadcasted_iota(jnp.int32, (n, n), 0)
        column = lax.broadcasted_iota(jnp.int32, (n, n), 1)
        half = n // 2
        from_row = jnp.where(row < half, 2 * row, 2 * (row - half) + 1)
        from_column = jnp.where(column < half, 2 * column, 2 * (column - half) + 1)
        left = jnp.where(column == from_row, 1.0, 0.0).astype(bf16)
        right = jnp.where(row == from_column, 1.0, 0.0).astype(bf16)

        def reorder(x):
            for side in (0, 1):
                total = None
                for _ in range(3):
                    part = x.astype(bf16)
                    x = x - part.astype(f32)
                    pair = (left, part) if side == 0 else (part, right)
                    moved = jnp.dot(*pair, preferred_element_type=f32)
                    total = moved if total is None else total + moved
                x = total
            return x

        angle = reorder(phase[...])
        copies = [pltpu.make_async_copy(held.at[i], out, sem.at[i]) for i, out in enumerate(outs)]
        values = [lambda: jnp.cos(angle), lambda: jnp.sin(angle)] + [lambda x=x: reorder(x[0]) for x in observed]
        for i, value in enumerate(values):
            held[i] = value()
            copies[i].start()
        for copy in copies:
            copy.wait()

    count = 2 + len(patterns)
    return pl.pallas_call(
        kernel,
        out_shape=[pltpu.HBM((n, n), f32)] * count,
        in_specs=[VMEM] * (1 + len(patterns)),
        out_specs=[ANY] * count,
        scratch_shapes=[pltpu.VMEM((count, n, n), f32), pltpu.SemaphoreType.DMA((count,))],
        compiler_params=PARAMS,
        cost_estimate=pl.CostEstimate(flops=36 * n**3, bytes_accessed=30 * n * n, transcendentals=2 * n * n),
    )(prop_phase, *patterns)


def run_forward(s, before, patch, after, cosine, sine, tables):
    re, im = times(before[0], before[1], patch[0], patch[1])
    a, b = forward(re, im, tables)
    a, b = by_phase(a, b, cosine[...], sine[...])
    re, im = inverse(a, b, tables)
    after[0] = re
    after[1] = im


def start_chunks(sources, patch, slot, sem):
    top = 0
    for source in sources:
        rows = source.shape[1]
        pltpu.make_async_copy(source, patch.at[slot, :, pl.ds(top, rows), :], sem).start()
        top += rows


def wait_slot(patch, slot, sem):
    pltpu.make_async_copy(patch.at[slot], patch.at[slot], sem).wait()


def fetch_patches(me, sources, patch, sems):
    for i, chunks in enumerate(sources):
        start_chunks(chunks, patch, me ^ i, sems.at[me ^ i])


def grouped(refs, patches, chunks):
    return [refs[i * chunks : (i + 1) * chunks] for i in range(patches)], refs[patches * chunks :]


def early_waves(cut, patches, probe, cosine, sine, tables):
    n = probe.shape[1]
    chunks = len(patches[0])

    def kernel(cut_ref, *refs):
        sources, rest = grouped(refs, 2, chunks)
        probe, cosine, sine, right, left, waves, patch, first, phase, sems, phase_sem = rest
        me = cut_ref[0]
        pairs = ((probe, first), (cosine, phase.at[0]), (sine, phase.at[1]))
        copies = [pltpu.make_async_copy(x, y, phase_sem.at[i]) for i, (x, y) in enumerate(pairs)]

        @pl.when(me < 2)
        def _():
            fetch_patches(me, sources, patch, sems)
            for copy in copies:
                copy.start()
            before = first
            for s in range(2):
                wait_slot(patch, s, sems.at[s])
                if s == 0:
                    for copy in copies:
                        copy.wait()
                run_forward(s, before, patch.at[s], waves.at[s], phase.at[0], phase.at[1], (right, left))
                before = waves.at[s]

    return pl.pallas_call(
        kernel,
        out_shape=jax.ShapeDtypeStruct((2, 2, n, n), f32),
        in_specs=[SMEM] + [ANY] * (2 * chunks + 3) + [VMEM] * 2,
        out_specs=VMEM,
        scratch_shapes=[
            pltpu.VMEM((2, 2, n, n), f32),
            pltpu.VMEM((2, n, n), f32),
            pltpu.VMEM((2, n, n), f32),
            pltpu.SemaphoreType.DMA((2,)),
            pltpu.SemaphoreType.DMA((3,)),
        ],
        compiler_params=PARAMS,
        cost_estimate=SHORT,
    )(cut, *flatten(patches[:2]), *map(pinned, (probe, cosine, sine)), *tables)


def flatten(patches):
    return [chunk for patch in patches for chunk in patch]


def chain(cut, patches, early, probe, cosine, sine, observed, tables):
    n = probe.shape[1]
    sections = len(patches)
    chunks = len(patches[0])
    planes_in = [cosine, sine, observed, probe, early]

    def kernel(cut_ref, *refs):
        sources, rest = grouped(refs, sections, chunks)
        *planes, right, left, out, patch, waves, held, probe, sems, early_sem, held_sem = rest
        me = cut_ref[0]
        tables = (right, left)
        targets = [held.at[0], held.at[1], held.at[2], probe]
        copies = [pltpu.make_async_copy(x, y, held_sem.at[i]) for i, (x, y) in enumerate(zip(planes, targets))]
        cosine, sine, observed = [held.at[i] for i in range(3)]

        def wave(s):
            return probe if s == 0 else waves.at[s - 1]

        def first_two():
            for s in range(2):
                run_forward(s, wave(s), patch.at[s], waves.at[s], cosine, sine, tables)

        def back(s, re, im):
            @pl.when(me == s)
            def _():
                out[0], out[1] = conj_times(wave(s)[0], wave(s)[1], re, im)

            if s > 0:

                @pl.when(me < s)
                def _():
                    gr, gi = conj_times(patch[s, 0], patch[s, 1], re, im)
                    a, b = forward(gr, gi, tables)
                    a, b = by_phase(a, b, cosine[...], -sine[...])
                    back(s - 1, *inverse(a, b, tables))

        early_copy = pltpu.make_async_copy(planes[4], waves.at[pl.ds(0, 2)], early_sem)

        @pl.when(me < 2)
        def _():
            early_copy.start()

        fetch_patches(me, sources, patch, sems)
        for copy in copies:
            copy.start()
        for s in range(2):
            wait_slot(patch, s, sems.at[s])
        for copy in (copies[0], copies[1], copies[3]):
            copy.wait()

        @pl.when(me < 2)
        def _():
            early_copy.wait()

        pl.when(me >= 2)(first_two)
        for s in range(2, sections):
            wait_slot(patch, s, sems.at[s])
            if s < sections - 1:
                run_forward(s, wave(s), patch.at[s], waves.at[s], cosine, sine, tables)
        copies[2].wait()
        last = sections - 1
        re, im = times(wave(last)[0], wave(last)[1], patch[last, 0], patch[last, 1])
        a, b = forward(re, im, tables)
        a, b = by_residual(a, b, observed[...])
        back(last, *inverse(a, b, tables))

    return pl.pallas_call(
        kernel,
        out_shape=jax.ShapeDtypeStruct((2, n, n), f32),
        in_specs=[SMEM] + [ANY] * (sections * chunks + len(planes_in)) + [VMEM] * 2,
        out_specs=VMEM,
        scratch_shapes=[
            pltpu.VMEM((sections, 2, n, n), f32),
            pltpu.VMEM((sections - 1, 2, n, n), f32),
            pltpu.VMEM((3, n, n), f32),
            pltpu.VMEM((2, n, n), f32),
            pltpu.SemaphoreType.DMA((sections,)),
            pltpu.SemaphoreType.DMA,
            pltpu.SemaphoreType.DMA((4,)),
        ],
        compiler_params=PARAMS,
        cost_estimate=pl.CostEstimate(flops=10 * 24 * n**3, bytes_accessed=16 * n * n, transcendentals=0),
    )(cut, *flatten(patches), *map(pinned, (cosine, sine, observed, probe)), early, *tables)


def window_start(column, width, columns):
    start = jnp.minimum(column // LANE * LANE, columns - width - LANE)
    return pl.multiple_of(start, LANE), column - start


def packed(row_off, col_off):
    def kernel(row_off, col_off, out):
        out[0] = row_off[0]
        out[1] = col_off[0]

    return pl.pallas_call(
        kernel,
        out_shape=jax.ShapeDtypeStruct((2,), jnp.int32),
        in_specs=[SMEM, SMEM],
        out_specs=SMEM,
        compiler_params=PARAMS,
    )(row_off, col_off)


def cut_window(offsets, strip, width, bounds):
    _, _, rows, columns = strip.shape
    chunks = len(bounds) - 1

    def kernel(offsets, strip, *refs):
        outs, (wide, sem) = refs[:chunks], refs[chunks:]
        row, column = offsets[0], offsets[1]
        start, shift = window_start(column, width, columns)
        run = pl.ds(start, width + LANE)
        copies = [pltpu.make_async_copy(strip.at[0, c, :, run], wide.at[c], sem.at[c]) for c in range(2)]
        for copy in copies:
            copy.start()
        for c in range(2):
            copies[c].wait()
            x = pltpu.roll(wide[c], lax.rem(width + LANE - shift, width + LANE), 1)[:, :width]
            x = pltpu.roll(x, lax.rem(rows - row, rows), 0)
            for j in range(chunks):
                outs[j][c] = x[bounds[j] : bounds[j + 1]]

    return pl.pallas_call(
        kernel,
        out_shape=[jax.ShapeDtypeStruct((2, bounds[j + 1] - bounds[j], width), f32) for j in range(chunks)],
        in_specs=[SMEM, ANY],
        out_specs=[VMEM] * chunks,
        scratch_shapes=[pltpu.VMEM((2, rows, width + LANE), f32), pltpu.SemaphoreType.DMA((2,))],
        compiler_params=PARAMS,
    )(offsets, pinned(strip))


def moved(piece, row, shift, keep):
    rows = piece.shape[0]
    x = jnp.where(keep, pltpu.roll(piece, row, 0), 0.0)
    return pltpu.roll(jnp.concatenate([x, jnp.zeros((rows, LANE), f32)], 1), shift, 1)


def place_own(offsets, piece, columns):
    _, rows, width = piece.shape

    def kernel(offsets, piece, out):
        index = lax.broadcasted_iota(jnp.int32, (rows, width), 0)
        out[...] = jnp.zeros_like(out)
        row = offsets[0]
        start, shift = window_start(offsets[1], width, columns)
        for c in range(2):
            out[0, c, :, pl.ds(start, width + LANE)] = moved(piece[c], row, shift, index >= row)

    return pl.pallas_call(
        kernel,
        out_shape=jax.ShapeDtypeStruct((1, 2, rows, columns), f32),
        in_specs=[SMEM, VMEM],
        out_specs=VMEM,
        compiler_params=PARAMS,
    )(offsets, piece)


def add_came(offsets, came, base):
    _, rows, width = came.shape
    columns = base.shape[3]

    def kernel(offsets, came, base, out, wide, sem):
        row = offsets[0]
        start, shift = window_start(offsets[1], width, columns)
        run = pl.ds(start, width + LANE)
        reads = [pltpu.make_async_copy(base.at[0, c, :, run], wide.at[c], sem.at[c]) for c in range(2)]
        writes = [pltpu.make_async_copy(wide.at[c], out.at[0, c, :, run], sem.at[c]) for c in range(2)]
        for copy in reads:
            copy.start()
        index = lax.broadcasted_iota(jnp.int32, (rows, width), 0)
        for c in range(2):
            x = moved(came[c], row, shift, index < row)
            reads[c].wait()
            wide[c] = wide[c] + x
            writes[c].start()
        for copy in writes:
            copy.wait()

    return pl.pallas_call(
        kernel,
        out_shape=jax.ShapeDtypeStruct(base.shape, f32),
        in_specs=[SMEM, VMEM, ANY],
        out_specs=ANY,
        input_output_aliases={2: 0},
        scratch_shapes=[pltpu.VMEM((2, rows, width + LANE), f32), pltpu.SemaphoreType.DMA((2,))],
        compiler_params=PARAMS,
    )(offsets, came, pinned(base))


def shifted(value, by):
    devices = lax.axis_size("tile")
    pairs = [(i, i + by) for i in range(devices) if 0 <= i + by < devices]
    return lax.ppermute(value, "tile", pairs)


def swapped(value, bit):
    devices = lax.axis_size("cuts")
    return lax.ppermute(value, "cuts", [(i, i ^ bit) for i in range(devices)])


def after(*values):
    return lax.optimization_barrier(values)


def merged(first, second, top, row, rows):
    index = lax.broadcasted_iota(jnp.int32, first.shape, 1) + top
    return jnp.where(index < rows - row, first, second)


BOUNDS = (0, 128, 256)


def per_device(transmission, probe, prop_phase, row_off, col_off, measured):
    rows, columns = transmission.shape[2:]
    width = probe.shape[1]
    cut = lax.axis_index("cuts").astype(jnp.int32).reshape(1)
    offsets = packed(row_off, col_off)
    came_offsets = shifted(offsets, 1)
    below = [shifted(band, -1) for band in cut_window(came_offsets, transmission, width, BOUNDS)]
    own = cut_window(offsets, transmission, width, BOUNDS)
    cosine, sine, observed = prepare(prop_phase, measured)
    tables = [jnp.asarray(t) for t in dft_tables(width)]

    chunks, across = [], []
    for j, (first, second) in enumerate(zip(own, below)):
        if chunks:
            first, second, chunks[-1], cosine = after(first, second, chunks[-1], cosine)
        chunks.append(merged(first, second, BOUNDS[j], row_off[0], rows))
        chunk = chunks[-1]
        across.append(swapped(chunk, 2))
    across[0], *later = after(across[0], *chunks)
    beside = [swapped(chunk, 1) for chunk in later]
    early = early_waves(cut, [chunks, beside], probe, cosine, sine, tables)
    *across, early = after(*across, early)
    opposite = [swapped(chunk, 1) for chunk in across]
    piece = chain(cut, [chunks, beside, across, opposite], early, probe, cosine, sine, observed, tables)

    came = shifted(piece, 1)
    return add_came(came_offsets, came, place_own(offsets, piece, columns))


def solution(mesh):
    placed = (P("cuts", None, "tile", None), P(), P(), P("tile"), P("tile"), P("tile", None, None))
    return jax.shard_map(
        per_device,
        mesh=mesh,
        in_specs=placed,
        out_specs=P("cuts", None, "tile", None),
        check_vma=False,
    )
```

```python
import jax
import jax.numpy as jnp
import numpy as np
from jax import lax
from jax.experimental import pallas as pl
from jax.experimental.pallas import tpu as pltpu
from jax.sharding import PartitionSpec as P

f32, bf16 = jnp.float32, jnp.bfloat16
LANE = 128
VMEM = pl.BlockSpec(memory_space=pltpu.VMEM)
SMEM = pl.BlockSpec(memory_space=pltpu.SMEM)
ANY = pl.BlockSpec(memory_space=pl.ANY)
HBM = pl.BlockSpec(memory_space=pltpu.HBM)
SHORT = pl.CostEstimate(flops=1 << 16, bytes_accessed=1 << 12, transcendentals=0)
PARAMS = pltpu.CompilerParams(vmem_limit_bytes=12 << 20)


def dft_tables(n):
    half = n // 2
    k = np.arange(half)[:, None]
    m = np.arange(half)[None, :]

    def real_form(odd):
        angle = -2 * np.pi * ((k * (2 * m + odd)) % n) / n
        c, s = np.cos(angle) / np.sqrt(n), np.sin(angle) / np.sqrt(n)
        return np.block([[c, s], [-s, c]])

    def parts(matrix, axis):
        high = matrix.astype(np.float32).astype(jnp.bfloat16)
        low = (matrix - high.astype(np.float64)).astype(np.float32).astype(jnp.bfloat16)
        return np.concatenate([high, high, low], axis=axis)

    even, odd = real_form(0), real_form(1)
    right = np.stack([parts(m, 0) for m in (even, odd, even.T, odd.T)])
    left = np.stack([parts(m, 1) for m in (even.T, odd.T, even, odd)])
    return right, left


def pinned(x):
    return pltpu.with_memory_space_constraint(x, pltpu.HBM)


def split(x, axis):
    high = x.astype(bf16)
    low = (x - high.astype(f32)).astype(bf16)
    return jnp.concatenate([high, low, high], axis=axis)


def right_dot(x, table):
    return jnp.dot(split(x, 1), table, preferred_element_type=f32)


def left_dot(table, x):
    return jnp.dot(table, split(x, 0), preferred_element_type=f32)


def to_rows(a, b):
    h = a.shape[0] // 2

    def one(r):
        re = jnp.concatenate([a[r : r + h, :h], b[r : r + h, :h]], 1)
        im = jnp.concatenate([a[r : r + h, h:], b[r : r + h, h:]], 1)
        return jnp.concatenate([re, im], 0)

    return one(0), one(h)


def to_columns(a, b):
    h = a.shape[0] // 2

    def one(c):
        top = jnp.concatenate([a[:h, c : c + h], a[h:, c : c + h]], 1)
        bottom = jnp.concatenate([b[:h, c : c + h], b[h:, c : c + h]], 1)
        return jnp.concatenate([top, bottom], 0)

    return one(0), one(h)


def columns_of(re, im):
    h = re.shape[1] // 2
    return (
        jnp.concatenate([re[:, :h], im[:, :h]], 1),
        jnp.concatenate([re[:, h:], im[:, h:]], 1),
    )


def planes_of(a, b):
    h = a.shape[1] // 2
    return (
        jnp.concatenate([a[:, :h], b[:, :h]], 1),
        jnp.concatenate([a[:, h:], b[:, h:]], 1),
    )


def forward(re, im, tables):
    right, left = tables
    a, b = columns_of(re, im)
    a, b = to_rows(right_dot(a + b, right[0]), right_dot(a - b, right[1]))
    return left_dot(left[0], a + b), left_dot(left[1], a - b)


def inverse(a, b, tables):
    right, left = tables
    p, q = left_dot(left[2], a), left_dot(left[3], b)
    a, b = to_columns(p + q, p - q)
    p, q = right_dot(a, right[2]), right_dot(b, right[3])
    return planes_of(p + q, p - q)


def times(ar, ai, br, bi):
    return ar * br - ai * bi, ar * bi + ai * br


def conj_times(ar, ai, br, bi):
    return ar * br + ai * bi, ar * bi - ai * br


def by_phase(a, b, cosine, sine):
    h = a.shape[0] // 2
    out = []
    for i, x in enumerate((a, b)):
        at = slice(i * h, (i + 1) * h)
        re, im = times(x[:h], x[h:], cosine[at], sine[at])
        out.append(jnp.concatenate([re, im], 0))
    return out


def by_residual(a, b, observed):
    h = a.shape[0] // 2
    out = []
    for i, x in enumerate((a, b)):
        re, im = x[:h], x[h:]
        residual = re * re + im * im - observed[i * h : (i + 1) * h]
        out.append(jnp.concatenate([residual * re, residual * im], 0))
    return out


def prepare(prop_phase, *patterns):
    n = prop_phase.shape[0]

    def kernel(phase, *refs):
        observed, outs, (held, sem) = refs[: len(patterns)], refs[len(patterns) : -2], refs[-2:]
        row = lax.broadcasted_iota(jnp.int32, (n, n), 0)
        column = lax.broadcasted_iota(jnp.int32, (n, n), 1)
        half = n // 2
        from_row = jnp.where(row < half, 2 * row, 2 * (row - half) + 1)
        from_column = jnp.where(column < half, 2 * column, 2 * (column - half) + 1)
        left = jnp.where(column == from_row, 1.0, 0.0).astype(bf16)
        right = jnp.where(row == from_column, 1.0, 0.0).astype(bf16)

        def reorder(x):
            for side in (0, 1):
                total = None
                for _ in range(3):
                    part = x.astype(bf16)
                    x = x - part.astype(f32)
                    pair = (left, part) if side == 0 else (part, right)
                    moved = jnp.dot(*pair, preferred_element_type=f32)
                    total = moved if total is None else total + moved
                x = total
            return x

        angle = reorder(phase[...])
        copies = [pltpu.make_async_copy(held.at[i], out, sem.at[i]) for i, out in enumerate(outs)]
        values = [lambda: jnp.cos(angle), lambda: jnp.sin(angle)] + [lambda x=x: reorder(x[0]) for x in observed]
        for i, value in enumerate(values):
            held[i] = value()
            copies[i].start()
        for copy in copies:
            copy.wait()

    count = 2 + len(patterns)
    return pl.pallas_call(
        kernel,
        out_shape=[pltpu.HBM((n, n), f32)] * count,
        in_specs=[VMEM] * (1 + len(patterns)),
        out_specs=[ANY] * count,
        scratch_shapes=[pltpu.VMEM((count, n, n), f32), pltpu.SemaphoreType.DMA((count,))],
        compiler_params=PARAMS,
        cost_estimate=pl.CostEstimate(flops=36 * n**3, bytes_accessed=30 * n * n, transcendentals=2 * n * n),
    )(prop_phase, *patterns)


def run_forward(s, before, patch, after, cosine, sine, tables):
    re, im = times(before[0], before[1], patch[0], patch[1])
    a, b = forward(re, im, tables)
    a, b = by_phase(a, b, cosine[...], sine[...])
    re, im = inverse(a, b, tables)
    after[0] = re
    after[1] = im


def start_chunks(sources, patch, slot, sem):
    top = 0
    for source in sources:
        rows = source.shape[1]
        pltpu.make_async_copy(source, patch.at[slot, :, pl.ds(top, rows), :], sem).start()
        top += rows


def wait_slot(patch, slot, sem):
    pltpu.make_async_copy(patch.at[slot], patch.at[slot], sem).wait()


def fetch_patches(me, sources, patch, sems, which):
    for i in which:
        start_chunks(sources[i], patch, me ^ i, sems.at[me ^ i])


def grouped(refs, patches, chunks):
    return [refs[i * chunks : (i + 1) * chunks] for i in range(patches)], refs[patches * chunks :]


def early_waves(cut, patches, probe, cosine, sine, tables):
    n = probe.shape[1]
    chunks = len(patches[0])

    def kernel(cut_ref, *refs):
        sources, rest = grouped(refs, 2, chunks)
        probe, cosine, sine, right, left, waves, patch, first, phase, sems, phase_sem = rest
        me = cut_ref[0]
        pairs = ((probe, first), (cosine, phase.at[0]), (sine, phase.at[1]))
        copies = [pltpu.make_async_copy(x, y, phase_sem.at[i]) for i, (x, y) in enumerate(pairs)]

        @pl.when(me < 2)
        def _():
            fetch_patches(me, sources, patch, sems, (0, 1))
            for copy in copies:
                copy.start()
            before = first
            for s in range(2):
                wait_slot(patch, s, sems.at[s])
                if s == 0:
                    for copy in copies:
                        copy.wait()
                run_forward(s, before, patch.at[s], waves.at[s], phase.at[0], phase.at[1], (right, left))
                before = waves.at[s]

    return pl.pallas_call(
        kernel,
        out_shape=jax.ShapeDtypeStruct((2, 2, n, n), f32),
        in_specs=[SMEM] + [ANY] * (2 * chunks + 3) + [VMEM] * 2,
        out_specs=VMEM,
        scratch_shapes=[
            pltpu.VMEM((2, 2, n, n), f32),
            pltpu.VMEM((2, n, n), f32),
            pltpu.VMEM((2, n, n), f32),
            pltpu.SemaphoreType.DMA((2,)),
            pltpu.SemaphoreType.DMA((3,)),
        ],
        compiler_params=PARAMS,
        cost_estimate=SHORT,
    )(cut, *flatten(patches[:2]), *map(pinned, (probe, cosine, sine)), *tables)


def flatten(patches):
    return [chunk for patch in patches for chunk in patch]


def chain(cut, patches, early, probe, cosine, sine, observed, tables):
    n = probe.shape[1]
    sections = len(patches)
    chunks = len(patches[0])
    planes_in = [cosine, sine, observed, probe, early]

    def kernel(cut_ref, *refs):
        sources, rest = grouped(refs, sections, chunks)
        *planes, right, left, out_re, out_im, patch, waves, held, probe, sems, early_sem, held_sem = rest
        me = cut_ref[0]
        tables = (right, left)
        targets = [held.at[0], held.at[1], held.at[2], probe]
        copies = [pltpu.make_async_copy(x, y, held_sem.at[i]) for i, (x, y) in enumerate(zip(planes, targets))]
        cosine, sine, observed = [held.at[i] for i in range(3)]

        def wave(s):
            return probe if s == 0 else waves.at[s - 1]

        def first_two():
            for s in range(2):
                run_forward(s, wave(s), patch.at[s], waves.at[s], cosine, sine, tables)

        def back(s, re, im):
            @pl.when(me == s)
            def _():
                out_re[...], out_im[...] = conj_times(wave(s)[0], wave(s)[1], re, im)

            if s > 0:

                @pl.when(me < s)
                def _():
                    gr, gi = conj_times(patch[s, 0], patch[s, 1], re, im)
                    a, b = forward(gr, gi, tables)
                    a, b = by_phase(a, b, cosine[...], -sine[...])
                    back(s - 1, *inverse(a, b, tables))

        early_copy = pltpu.make_async_copy(planes[4], waves.at[pl.ds(0, 2)], early_sem)

        fetch_patches(me, sources, patch, sems, (2, 3))

        @pl.when(me < 2)
        def _():
            early_copy.start()

        for copy in copies:
            copy.start()
        fetch_patches(me, sources, patch, sems, (0, 1))
        for copy in copies[:2]:
            copy.wait()

        @pl.when(me < 2)
        def _():
            early_copy.wait()

        @pl.when(me >= 2)
        def _():
            copies[3].wait()
            for s in range(2):
                wait_slot(patch, s, sems.at[s])
            first_two()

        for s in range(2, sections):
            wait_slot(patch, s, sems.at[s])
            if s < sections - 1:
                run_forward(s, wave(s), patch.at[s], waves.at[s], cosine, sine, tables)
        copies[2].wait()

        @pl.when(me < 2)
        def _():
            copies[3].wait()
            for s in range(2):
                wait_slot(patch, s, sems.at[s])

        last = sections - 1
        re, im = times(wave(last)[0], wave(last)[1], patch[last, 0], patch[last, 1])
        a, b = forward(re, im, tables)
        a, b = by_residual(a, b, observed[...])
        back(last, *inverse(a, b, tables))

    return pl.pallas_call(
        kernel,
        out_shape=[jax.ShapeDtypeStruct((n, n), f32)] * 2,
        in_specs=[SMEM] + [ANY] * (sections * chunks + len(planes_in)) + [VMEM] * 2,
        out_specs=[VMEM] * 2,
        scratch_shapes=[
            pltpu.VMEM((sections, 2, n, n), f32),
            pltpu.VMEM((sections - 1, 2, n, n), f32),
            pltpu.VMEM((3, n, n), f32),
            pltpu.VMEM((2, n, n), f32),
            pltpu.SemaphoreType.DMA((sections,)),
            pltpu.SemaphoreType.DMA,
            pltpu.SemaphoreType.DMA((4,)),
        ],
        compiler_params=PARAMS,
        cost_estimate=pl.CostEstimate(flops=10 * 24 * n**3, bytes_accessed=16 * n * n, transcendentals=0),
    )(cut, *flatten(patches), *map(pinned, (cosine, sine, observed, probe)), early, *tables)


def window_start(column, width, columns):
    start = jnp.minimum(column // LANE * LANE, columns - width - LANE)
    return pl.multiple_of(start, LANE), column - start


def packed(row_off, col_off):
    def kernel(row_off, col_off, out):
        out[0] = row_off[0]
        out[1] = col_off[0]

    return pl.pallas_call(
        kernel,
        out_shape=jax.ShapeDtypeStruct((2,), jnp.int32),
        in_specs=[SMEM, SMEM],
        out_specs=SMEM,
        compiler_params=PARAMS,
    )(row_off, col_off)


def cut_window(offsets, strip, width, bounds):
    _, _, rows, columns = strip.shape
    chunks = len(bounds) - 1

    def kernel(offsets, strip, *refs):
        outs, (wide, sem) = refs[:chunks], refs[chunks:]
        row, column = offsets[0], offsets[1]
        start, shift = window_start(column, width, columns)
        run = pl.ds(start, width + LANE)
        copies = [pltpu.make_async_copy(strip.at[0, c, :, run], wide.at[c], sem.at[c]) for c in range(2)]
        for copy in copies:
            copy.start()
        for c in range(2):
            copies[c].wait()
            x = pltpu.roll(wide[c], lax.rem(width + LANE - shift, width + LANE), 1)[:, :width]
            x = pltpu.roll(x, lax.rem(rows - row, rows), 0)
            for j in range(chunks):
                outs[j][c] = x[bounds[j] : bounds[j + 1]]

    return pl.pallas_call(
        kernel,
        out_shape=[jax.ShapeDtypeStruct((2, bounds[j + 1] - bounds[j], width), f32) for j in range(chunks)],
        in_specs=[SMEM, ANY],
        out_specs=[VMEM] * chunks,
        scratch_shapes=[pltpu.VMEM((2, rows, width + LANE), f32), pltpu.SemaphoreType.DMA((2,))],
        compiler_params=PARAMS,
    )(offsets, pinned(strip))


def moved(piece, row, shift, keep):
    rows = piece.shape[0]
    x = jnp.where(keep, pltpu.roll(piece, row, 0), 0.0)
    return pltpu.roll(jnp.concatenate([x, jnp.zeros((rows, LANE), f32)], 1), shift, 1)


def place_own(offsets, came_offsets, planes, columns):
    rows, width = planes[0].shape

    def kernel(offsets, came_offsets, re, im, out, *runs):
        index = lax.broadcasted_iota(jnp.int32, (rows, width), 0)
        out[...] = jnp.zeros_like(out)
        row = offsets[0]
        start, shift = window_start(offsets[1], width, columns)
        came_start, _ = window_start(came_offsets[1], width, columns)
        for c, plane in enumerate((re, im)):
            out[0, c, :, pl.ds(start, width + LANE)] = moved(plane[...], row, shift, index >= row)
            runs[c][...] = out[0, c, :, pl.ds(came_start, width + LANE)]

    return pl.pallas_call(
        kernel,
        out_shape=[jax.ShapeDtypeStruct((1, 2, rows, columns), f32)] + [pltpu.VMEM((rows, width + LANE), f32)] * 2,
        in_specs=[SMEM, SMEM, VMEM, VMEM],
        out_specs=[VMEM] * 3,
        compiler_params=PARAMS,
    )(offsets, came_offsets, *planes)


def add_came(offsets, came, run, base, c):
    rows, width = came.shape
    columns = base.shape[3]

    def kernel(offsets, came, run, base, out, wide, sem):
        row = offsets[0]
        start, shift = window_start(offsets[1], width, columns)
        index = lax.broadcasted_iota(jnp.int32, (rows, width), 0)
        wide[...] = run[...] + moved(came[...], row, shift, index < row)
        write = pltpu.make_async_copy(wide, out.at[0, c, :, pl.ds(start, width + LANE)], sem)
        write.start()
        write.wait()

    return pl.pallas_call(
        kernel,
        out_shape=jax.ShapeDtypeStruct(base.shape, f32),
        in_specs=[SMEM, VMEM, VMEM, ANY],
        out_specs=ANY,
        input_output_aliases={3: 0},
        scratch_shapes=[pltpu.VMEM((rows, width + LANE), f32), pltpu.SemaphoreType.DMA],
        compiler_params=PARAMS,
    )(offsets, came, run, pinned(base))


def shifted(value, by):
    devices = lax.axis_size("tile")
    pairs = [(i, i + by) for i in range(devices) if 0 <= i + by < devices]
    return lax.ppermute(value, "tile", pairs)


def swapped(value, bit):
    devices = lax.axis_size("cuts")
    return lax.ppermute(value, "cuts", [(i, i ^ bit) for i in range(devices)])


def after(*values):
    return lax.optimization_barrier(values)


def merged(first, second, top, row, rows):
    index = lax.broadcasted_iota(jnp.int32, first.shape, 1) + top
    return jnp.where(index < rows - row, first, second)


BOUNDS = (0, 128, 256)


def per_device(transmission, probe, prop_phase, row_off, col_off, measured):
    rows, columns = transmission.shape[2:]
    width = probe.shape[1]
    cut = lax.axis_index("cuts").astype(jnp.int32).reshape(1)
    offsets = packed(row_off, col_off)
    came_offsets = shifted(offsets, 1)
    cosine, sine, observed = prepare(prop_phase, measured)
    bands = list(cut_window(came_offsets, transmission, width, BOUNDS))
    below = [shifted(band, -1) for band in bands]
    own = cut_window(offsets, transmission, width, BOUNDS)
    tables = [jnp.asarray(t) for t in dft_tables(width)]

    chunks, across = [], []
    below[0], cosine, sine, observed = after(below[0], cosine, sine, observed)
    for j, (first, second) in enumerate(zip(own, below)):
        if chunks:
            first, second, chunks[-1] = after(first, second, chunks[-1])
        chunks.append(merged(first, second, BOUNDS[j], row_off[0], rows))
        chunk = chunks[-1]
        across.append(swapped(chunk, 2))
    beside = [swapped(chunk, 1) for chunk in chunks]
    across[0], beside[0] = after(across[0], beside[0])
    early = early_waves(cut, [chunks, beside], probe, cosine, sine, tables)
    across[1], early = after(across[1], early)
    opposite = [swapped(chunk, 1) for chunk in across]
    planes = chain(cut, [chunks, beside, across, opposite], early, probe, cosine, sine, observed, tables)

    came = [shifted(plane, 1) for plane in planes]
    gradient, *runs = place_own(offsets, came_offsets, planes, columns)
    for c in range(2):
        gradient = add_came(came_offsets, came[c], runs[c], gradient, c)
    return gradient


def solution(mesh):
    placed = (P("cuts", None, "tile", None), P(), P(), P("tile"), P("tile"), P("tile", None, None))
    return jax.shard_map(
        per_device,
        mesh=mesh,
        in_specs=placed,
        out_specs=P("cuts", None, "tile", None),
        check_vma=False,
    )
```

```python
import jax
import jax.numpy as jnp
import numpy as np
from jax import lax
from jax.experimental import pallas as pl
from jax.experimental.pallas import tpu as pltpu
from jax.sharding import PartitionSpec as P

f32, bf16 = jnp.float32, jnp.bfloat16
LANE = 128
VMEM = pl.BlockSpec(memory_space=pltpu.VMEM)
SMEM = pl.BlockSpec(memory_space=pltpu.SMEM)
ANY = pl.BlockSpec(memory_space=pl.ANY)
HBM = pl.BlockSpec(memory_space=pltpu.HBM)
SHORT = pl.CostEstimate(flops=1 << 16, bytes_accessed=1 << 12, transcendentals=0)
PARAMS = pltpu.CompilerParams(vmem_limit_bytes=12 << 20)


def dft_tables(n):
    def real_form(radix, first):
        k = np.arange(n // radix)[:, None]
        m = np.arange(n // radix)[None, :]
        angle = -2 * np.pi * ((k * (radix * m + first)) % n) / n
        c, s = np.cos(angle) / np.sqrt(n), np.sin(angle) / np.sqrt(n)
        return np.block([[c, s], [-s, c]])

    def parts(matrix):
        high = matrix.astype(np.float32).astype(jnp.bfloat16)
        low = (matrix - high.astype(np.float64)).astype(np.float32).astype(jnp.bfloat16)
        return high, low

    def for_right(matrix):
        high, low = parts(matrix)
        return np.concatenate([high, high, low], axis=0)

    def for_left(matrix):
        high, low = parts(matrix)
        return np.block([[high, high], [low, np.zeros_like(low)]])

    halves = [real_form(2, first) for first in range(2)]
    quarters = [real_form(4, first) for first in range(4)]
    right = np.stack([for_right(m) for m in halves + [m.T for m in halves]])
    left = np.stack([for_left(m) for m in [m.T for m in quarters] + quarters])
    return right, left


def pinned(x):
    return pltpu.with_memory_space_constraint(x, pltpu.HBM)


def split(x):
    high = x.astype(bf16)
    return high, (x - high.astype(f32)).astype(bf16)


def right_dot(x, table):
    high, low = split(x)
    return jnp.dot(jnp.concatenate([high, low, high], 1), table, preferred_element_type=f32)


def left_dot(table, x):
    both = jnp.dot(table, jnp.concatenate(split(x), 0), preferred_element_type=f32)
    h = both.shape[0] // 2
    return both[:h] + both[h:]


def columns_of(re, im):
    h = re.shape[1] // 2
    return (
        jnp.concatenate([re[:, :h], im[:, :h]], 1),
        jnp.concatenate([re[:, h:], im[:, h:]], 1),
    )


def planes_of(a, b):
    h = a.shape[1] // 2
    return (
        jnp.concatenate([a[:, :h], b[:, :h]], 1),
        jnp.concatenate([a[:, h:], b[:, h:]], 1),
    )


def forward(re, im, tables):
    right, left = tables
    a, b = columns_of(re, im)
    re, im = planes_of(right_dot(a + b, right[0]), right_dot(a - b, right[1]))
    q = re.shape[0] // 4
    (r0, r1, r2, r3), (i0, i1, i2, i3) = [[x[j * q : (j + 1) * q] for j in range(4)] for x in (re, im)]
    pr, pi, ur, ui = r0 + r2, i0 + i2, r0 - r2, i0 - i2
    qr, qi, vr, vi = r1 + r3, i1 + i3, r1 - r3, i1 - i3
    mixed = ((pr + qr, pi + qi), (ur + vi, ui - vr), (pr - qr, pi - qi), (ur - vi, ui + vr))
    return [left_dot(left[j], jnp.concatenate(x, 0)) for j, x in enumerate(mixed)]


def inverse(spectrum, tables):
    right, left = tables
    q = spectrum[0].shape[0] // 2
    parts = [left_dot(left[4 + j], x) for j, x in enumerate(spectrum)]
    (r0, i0), (r1, i1), (r2, i2), (r3, i3) = [(x[:q], x[q:]) for x in parts]
    ar, ai, br, bi = r0 + r2, i0 + i2, r0 - r2, i0 - i2
    cr, ci, dr, di = r1 + r3, i1 + i3, r1 - r3, i1 - i3
    re = jnp.concatenate([ar + cr, br - di, ar - cr, br + di], 0)
    im = jnp.concatenate([ai + ci, bi + dr, ai - ci, bi - dr], 0)
    a, b = columns_of(re, im)
    p, q = right_dot(a, right[2]), right_dot(b, right[3])
    return planes_of(p + q, p - q)


def times(ar, ai, br, bi):
    return ar * br - ai * bi, ar * bi + ai * br


def conj_times(ar, ai, br, bi):
    return ar * br + ai * bi, ar * bi - ai * br


def by_phase(spectrum, cosine, sine):
    q = spectrum[0].shape[0] // 2
    out = []
    for i, x in enumerate(spectrum):
        at = slice(i * q, (i + 1) * q)
        out.append(jnp.concatenate(times(x[:q], x[q:], cosine[at], sine[at]), 0))
    return out


def by_residual(spectrum, observed):
    q = spectrum[0].shape[0] // 2
    out = []
    for i, x in enumerate(spectrum):
        re, im = x[:q], x[q:]
        residual = re * re + im * im - observed[i * q : (i + 1) * q]
        out.append(jnp.concatenate([residual * re, residual * im], 0))
    return out


def prepare(prop_phase, *patterns):
    n = prop_phase.shape[0]

    def kernel(phase, *refs):
        observed, outs, (held, sem) = refs[: len(patterns)], refs[len(patterns) : -2], refs[-2:]
        row = lax.broadcasted_iota(jnp.int32, (n, n), 0)
        column = lax.broadcasted_iota(jnp.int32, (n, n), 1)
        from_row = row % (n // 4) * 4 + row // (n // 4)
        from_column = column % (n // 2) * 2 + column // (n // 2)
        left = jnp.where(column == from_row, 1.0, 0.0).astype(bf16)
        right = jnp.where(row == from_column, 1.0, 0.0).astype(bf16)

        def reorder(x):
            for side in (0, 1):
                total = None
                for _ in range(3):
                    part = x.astype(bf16)
                    x = x - part.astype(f32)
                    pair = (left, part) if side == 0 else (part, right)
                    moved = jnp.dot(*pair, preferred_element_type=f32)
                    total = moved if total is None else total + moved
                x = total
            return x

        angle = reorder(phase[...])
        copies = [pltpu.make_async_copy(held.at[i], out, sem.at[i]) for i, out in enumerate(outs)]
        values = [lambda: jnp.cos(angle), lambda: jnp.sin(angle)] + [lambda x=x: reorder(x[0]) for x in observed]
        for i, value in enumerate(values):
            held[i] = value()
            copies[i].start()
        for copy in copies:
            copy.wait()

    count = 2 + len(patterns)
    return pl.pallas_call(
        kernel,
        out_shape=[pltpu.HBM((n, n), f32)] * count,
        in_specs=[VMEM] * (1 + len(patterns)),
        out_specs=[ANY] * count,
        scratch_shapes=[pltpu.VMEM((count, n, n), f32), pltpu.SemaphoreType.DMA((count,))],
        compiler_params=PARAMS,
        cost_estimate=pl.CostEstimate(flops=36 * n**3, bytes_accessed=30 * n * n, transcendentals=2 * n * n),
    )(prop_phase, *patterns)


def run_forward(s, before, patch, after, cosine, sine, tables):
    re, im = times(before[0], before[1], patch[0], patch[1])
    spectrum = by_phase(forward(re, im, tables), cosine[...], sine[...])
    re, im = inverse(spectrum, tables)
    after[0] = re
    after[1] = im


def start_chunks(sources, patch, slot, sem):
    top = 0
    for source in sources:
        rows = source.shape[1]
        pltpu.make_async_copy(source, patch.at[slot, :, pl.ds(top, rows), :], sem).start()
        top += rows


def wait_slot(patch, slot, sem):
    pltpu.make_async_copy(patch.at[slot], patch.at[slot], sem).wait()


def fetch_patches(me, sources, patch, sems, which):
    for i in which:
        start_chunks(sources[i], patch, me ^ i, sems.at[me ^ i])


def grouped(refs, patches, chunks):
    return [refs[i * chunks : (i + 1) * chunks] for i in range(patches)], refs[patches * chunks :]


def early_waves(cut, patches, probe, cosine, sine, tables):
    n = probe.shape[1]
    chunks = len(patches[0])

    def kernel(cut_ref, *refs):
        sources, rest = grouped(refs, 2, chunks)
        probe, cosine, sine, right, left, waves, patch, first, phase, sems, phase_sem = rest
        me = cut_ref[0]
        pairs = ((probe, first), (cosine, phase.at[0]), (sine, phase.at[1]))
        copies = [pltpu.make_async_copy(x, y, phase_sem.at[i]) for i, (x, y) in enumerate(pairs)]

        @pl.when(me < 2)
        def _():
            fetch_patches(me, sources, patch, sems, (0, 1))
            for copy in copies:
                copy.start()
            before = first
            for s in range(2):
                wait_slot(patch, s, sems.at[s])
                if s == 0:
                    for copy in copies:
                        copy.wait()
                run_forward(s, before, patch.at[s], waves.at[s], phase.at[0], phase.at[1], (right, left))
                before = waves.at[s]

    return pl.pallas_call(
        kernel,
        out_shape=jax.ShapeDtypeStruct((2, 2, n, n), f32),
        in_specs=[SMEM] + [ANY] * (2 * chunks + 3) + [VMEM] * 2,
        out_specs=VMEM,
        scratch_shapes=[
            pltpu.VMEM((2, 2, n, n), f32),
            pltpu.VMEM((2, n, n), f32),
            pltpu.VMEM((2, n, n), f32),
            pltpu.SemaphoreType.DMA((2,)),
            pltpu.SemaphoreType.DMA((3,)),
        ],
        compiler_params=PARAMS,
        cost_estimate=SHORT,
    )(cut, *flatten(patches[:2]), *map(pinned, (probe, cosine, sine)), *tables)


def flatten(patches):
    return [chunk for patch in patches for chunk in patch]


def chain(cut, patches, early, probe, cosine, sine, observed, tables):
    n = probe.shape[1]
    sections = len(patches)
    chunks = len(patches[0])
    planes_in = [cosine, sine, observed, probe, early]

    def kernel(cut_ref, *refs):
        sources, rest = grouped(refs, sections, chunks)
        *planes, right, left, out_re, out_im, patch, waves, held, probe, sems, early_sem, held_sem = rest
        me = cut_ref[0]
        tables = (right, left)
        targets = [held.at[0], held.at[1], held.at[2], probe]
        copies = [pltpu.make_async_copy(x, y, held_sem.at[i]) for i, (x, y) in enumerate(zip(planes, targets))]
        cosine, sine, observed = [held.at[i] for i in range(3)]

        def wave(s):
            return probe if s == 0 else waves.at[s - 1]

        def first_two():
            for s in range(2):
                run_forward(s, wave(s), patch.at[s], waves.at[s], cosine, sine, tables)

        def back(s, re, im):
            @pl.when(me == s)
            def _():
                out_re[...], out_im[...] = conj_times(wave(s)[0], wave(s)[1], re, im)

            if s > 0:

                @pl.when(me < s)
                def _():
                    gr, gi = conj_times(patch[s, 0], patch[s, 1], re, im)
                    spectrum = by_phase(forward(gr, gi, tables), cosine[...], -sine[...])
                    back(s - 1, *inverse(spectrum, tables))

        early_copy = pltpu.make_async_copy(planes[4], waves.at[pl.ds(0, 2)], early_sem)

        fetch_patches(me, sources, patch, sems, (2, 3))

        @pl.when(me < 2)
        def _():
            early_copy.start()

        for copy in copies:
            copy.start()
        fetch_patches(me, sources, patch, sems, (0, 1))
        for copy in copies[:2]:
            copy.wait()

        @pl.when(me < 2)
        def _():
            early_copy.wait()

        @pl.when(me >= 2)
        def _():
            copies[3].wait()
            for s in range(2):
                wait_slot(patch, s, sems.at[s])
            first_two()

        for s in range(2, sections):
            wait_slot(patch, s, sems.at[s])
            if s < sections - 1:
                run_forward(s, wave(s), patch.at[s], waves.at[s], cosine, sine, tables)
        copies[2].wait()

        @pl.when(me < 2)
        def _():
            copies[3].wait()
            for s in range(2):
                wait_slot(patch, s, sems.at[s])

        last = sections - 1
        re, im = times(wave(last)[0], wave(last)[1], patch[last, 0], patch[last, 1])
        spectrum = by_residual(forward(re, im, tables), observed[...])
        back(last, *inverse(spectrum, tables))

    return pl.pallas_call(
        kernel,
        out_shape=[jax.ShapeDtypeStruct((n, n), f32)] * 2,
        in_specs=[SMEM] + [ANY] * (sections * chunks + len(planes_in)) + [VMEM] * 2,
        out_specs=[VMEM] * 2,
        scratch_shapes=[
            pltpu.VMEM((sections, 2, n, n), f32),
            pltpu.VMEM((sections - 1, 2, n, n), f32),
            pltpu.VMEM((3, n, n), f32),
            pltpu.VMEM((2, n, n), f32),
            pltpu.SemaphoreType.DMA((sections,)),
            pltpu.SemaphoreType.DMA,
            pltpu.SemaphoreType.DMA((4,)),
        ],
        compiler_params=PARAMS,
        cost_estimate=pl.CostEstimate(flops=10 * 24 * n**3, bytes_accessed=16 * n * n, transcendentals=0),
    )(cut, *flatten(patches), *map(pinned, (cosine, sine, observed, probe)), early, *tables)


def window_start(column, width, columns):
    start = jnp.minimum(column // LANE * LANE, columns - width - LANE)
    return pl.multiple_of(start, LANE), column - start


def packed(row_off, col_off):
    def kernel(row_off, col_off, out):
        out[0] = row_off[0]
        out[1] = col_off[0]

    return pl.pallas_call(
        kernel,
        out_shape=jax.ShapeDtypeStruct((2,), jnp.int32),
        in_specs=[SMEM, SMEM],
        out_specs=SMEM,
        compiler_params=PARAMS,
    )(row_off, col_off)


def staged(strip):
    def kernel(strip, out, sem):
        copy = pltpu.make_async_copy(strip, out, sem)
        copy.start()
        copy.wait()

    return pl.pallas_call(
        kernel,
        out_shape=pltpu.VMEM(strip.shape, f32),
        in_specs=[ANY],
        out_specs=VMEM,
        scratch_shapes=[pltpu.SemaphoreType.DMA],
        compiler_params=PARAMS,
    )(pinned(strip))


def cut_window(offsets, strip, width, bounds):
    _, _, rows, columns = strip.shape
    chunks = len(bounds) - 1

    def kernel(offsets, strip, *outs):
        row, column = offsets[0], offsets[1]
        start, shift = window_start(column, width, columns)
        for c in range(2):
            x = strip[0, c, :, pl.ds(start, width + LANE)]
            x = pltpu.roll(x, lax.rem(width + LANE - shift, width + LANE), 1)[:, :width]
            x = pltpu.roll(x, lax.rem(rows - row, rows), 0)
            for j in range(chunks):
                outs[j][c] = x[bounds[j] : bounds[j + 1]]

    return pl.pallas_call(
        kernel,
        out_shape=[jax.ShapeDtypeStruct((2, bounds[j + 1] - bounds[j], width), f32) for j in range(chunks)],
        in_specs=[SMEM, VMEM],
        out_specs=[VMEM] * chunks,
        compiler_params=PARAMS,
    )(offsets, strip)


def moved(piece, row, shift, keep):
    rows = piece.shape[0]
    x = jnp.where(keep, pltpu.roll(piece, row, 0), 0.0)
    return pltpu.roll(jnp.concatenate([x, jnp.zeros((rows, LANE), f32)], 1), shift, 1)


def place_own(offsets, came_offsets, planes, columns):
    rows, width = planes[0].shape

    def kernel(offsets, came_offsets, re, im, out, *runs):
        index = lax.broadcasted_iota(jnp.int32, (rows, width), 0)
        out[...] = jnp.zeros_like(out)
        row = offsets[0]
        start, shift = window_start(offsets[1], width, columns)
        came_start, _ = window_start(came_offsets[1], width, columns)
        for c, plane in enumerate((re, im)):
            out[0, c, :, pl.ds(start, width + LANE)] = moved(plane[...], row, shift, index >= row)
            runs[c][...] = out[0, c, :, pl.ds(came_start, width + LANE)]

    return pl.pallas_call(
        kernel,
        out_shape=[jax.ShapeDtypeStruct((1, 2, rows, columns), f32)] + [pltpu.VMEM((rows, width + LANE), f32)] * 2,
        in_specs=[SMEM, SMEM, VMEM, VMEM],
        out_specs=[VMEM] * 3,
        compiler_params=PARAMS,
    )(offsets, came_offsets, *planes)


def add_came(offsets, came, run, base, c):
    rows, width = came.shape
    columns = base.shape[3]

    def kernel(offsets, came, run, base, out, wide, sem):
        row = offsets[0]
        start, shift = window_start(offsets[1], width, columns)
        index = lax.broadcasted_iota(jnp.int32, (rows, width), 0)
        wide[...] = run[...] + moved(came[...], row, shift, index < row)
        write = pltpu.make_async_copy(wide, out.at[0, c, :, pl.ds(start, width + LANE)], sem)
        write.start()
        write.wait()

    return pl.pallas_call(
        kernel,
        out_shape=jax.ShapeDtypeStruct(base.shape, f32),
        in_specs=[SMEM, VMEM, VMEM, ANY],
        out_specs=ANY,
        input_output_aliases={3: 0},
        scratch_shapes=[pltpu.VMEM((rows, width + LANE), f32), pltpu.SemaphoreType.DMA],
        compiler_params=PARAMS,
    )(offsets, came, run, pinned(base))


def shifted(value, by):
    devices = lax.axis_size("tile")
    pairs = [(i, i + by) for i in range(devices) if 0 <= i + by < devices]
    return lax.ppermute(value, "tile", pairs)


def swapped(value, bit):
    devices = lax.axis_size("cuts")
    return lax.ppermute(value, "cuts", [(i, i ^ bit) for i in range(devices)])


def after(*values):
    return lax.optimization_barrier(values)


def merged(first, second, top, row, rows):
    index = lax.broadcasted_iota(jnp.int32, first.shape, 1) + top
    return jnp.where(index < rows - row, first, second)


BOUNDS = (0, 128, 256)


def per_device(transmission, probe, prop_phase, row_off, col_off, measured):
    rows, columns = transmission.shape[2:]
    width = probe.shape[1]
    cut = lax.axis_index("cuts").astype(jnp.int32).reshape(1)
    offsets = packed(row_off, col_off)
    strip = staged(transmission)
    came_offsets = shifted(offsets, 1)
    cosine, sine, observed = prepare(prop_phase, measured)
    bands = list(cut_window(came_offsets, strip, width, BOUNDS))
    below = [shifted(band, -1) for band in bands]
    own = cut_window(offsets, strip, width, BOUNDS)
    tables = [jnp.asarray(t) for t in dft_tables(width)]

    chunks, across = [], []
    below[0], cosine, sine, observed = after(below[0], cosine, sine, observed)
    for j, (first, second) in enumerate(zip(own, below)):
        if chunks:
            first, second, chunks[-1] = after(first, second, chunks[-1])
        chunks.append(merged(first, second, BOUNDS[j], row_off[0], rows))
        chunk = chunks[-1]
        across.append(swapped(chunk, 2))
    beside = [swapped(chunk, 1) for chunk in chunks]
    across[0], beside[0] = after(across[0], beside[0])
    early = early_waves(cut, [chunks, beside], probe, cosine, sine, tables)
    across[1], early = after(across[1], early)
    opposite = [swapped(chunk, 1) for chunk in across]
    planes = chain(cut, [chunks, beside, across, opposite], early, probe, cosine, sine, observed, tables)

    came = [shifted(plane, 1) for plane in planes]
    gradient, *runs = place_own(offsets, came_offsets, planes, columns)
    for c in range(2):
        gradient = add_came(came_offsets, came[c], runs[c], gradient, c)
    return gradient


def solution(mesh):
    placed = (P("cuts", None, "tile", None), P(), P(), P("tile"), P("tile"), P("tile", None, None))
    return jax.shard_map(
        per_device,
        mesh=mesh,
        in_specs=placed,
        out_specs=P("cuts", None, "tile", None),
        check_vma=False,
    )
```

```python
import jax
import jax.numpy as jnp
import numpy as np
from jax import lax
from jax.experimental import pallas as pl
from jax.experimental.pallas import tpu as pltpu
from jax.sharding import PartitionSpec as P

f32, bf16 = jnp.float32, jnp.bfloat16
LANE = 128
VMEM = pl.BlockSpec(memory_space=pltpu.VMEM)
SMEM = pl.BlockSpec(memory_space=pltpu.SMEM)
ANY = pl.BlockSpec(memory_space=pl.ANY)
HBM = pl.BlockSpec(memory_space=pltpu.HBM)
SHORT = pl.CostEstimate(flops=1 << 16, bytes_accessed=1 << 12, transcendentals=0)
PARAMS = pltpu.CompilerParams(vmem_limit_bytes=12 << 20)


def dft_tables(n):
    def real_form(radix, first):
        k = np.arange(n // radix)[:, None]
        m = np.arange(n // radix)[None, :]
        angle = -2 * np.pi * ((k * (radix * m + first)) % n) / n
        c, s = np.cos(angle) / np.sqrt(n), np.sin(angle) / np.sqrt(n)
        return np.block([[c, s], [-s, c]])

    def parts(matrix):
        high = matrix.astype(np.float32).astype(jnp.bfloat16)
        low = (matrix - high.astype(np.float64)).astype(np.float32).astype(jnp.bfloat16)
        return high, low

    def for_right(matrix):
        high, low = parts(matrix)
        return np.concatenate([high, high, low], axis=0)

    def for_left(matrix):
        high, low = parts(matrix)
        return np.block([[high, high], [low, np.zeros_like(low)]])

    halves = [real_form(2, first) for first in range(2)]
    quarters = [real_form(4, first) for first in range(4)]
    right = np.stack([for_right(m) for m in halves + [m.T for m in halves]])
    left = np.stack([for_left(m) for m in [m.T for m in quarters] + quarters])
    return right, left


def pinned(x):
    return pltpu.with_memory_space_constraint(x, pltpu.HBM)


def split(x):
    high = x.astype(bf16)
    return high, (x - high.astype(f32)).astype(bf16)


def right_dot(x, table):
    high, low = split(x)
    return jnp.dot(jnp.concatenate([high, low, high], 1), table, preferred_element_type=f32)


def left_dot(table, x):
    both = jnp.dot(table, jnp.concatenate(split(x), 0), preferred_element_type=f32)
    h = both.shape[0] // 2
    return both[:h] + both[h:]


def columns_of(re, im):
    h = re.shape[1] // 2
    return (
        jnp.concatenate([re[:, :h], im[:, :h]], 1),
        jnp.concatenate([re[:, h:], im[:, h:]], 1),
    )


def planes_of(a, b):
    h = a.shape[1] // 2
    return (
        jnp.concatenate([a[:, :h], b[:, :h]], 1),
        jnp.concatenate([a[:, h:], b[:, h:]], 1),
    )


def forward(re, im, tables):
    right, left = tables
    a, b = columns_of(re, im)
    re, im = planes_of(right_dot(a + b, right[0]), right_dot(a - b, right[1]))
    q = re.shape[0] // 4
    (r0, r1, r2, r3), (i0, i1, i2, i3) = [[x[j * q : (j + 1) * q] for j in range(4)] for x in (re, im)]
    pr, pi, ur, ui = r0 + r2, i0 + i2, r0 - r2, i0 - i2
    qr, qi, vr, vi = r1 + r3, i1 + i3, r1 - r3, i1 - i3
    mixed = ((pr + qr, pi + qi), (ur + vi, ui - vr), (pr - qr, pi - qi), (ur - vi, ui + vr))
    return [left_dot(left[j], jnp.concatenate(x, 0)) for j, x in enumerate(mixed)]


def inverse(spectrum, tables):
    right, left = tables
    q = spectrum[0].shape[0] // 2
    parts = [left_dot(left[4 + j], x) for j, x in enumerate(spectrum)]
    (r0, i0), (r1, i1), (r2, i2), (r3, i3) = [(x[:q], x[q:]) for x in parts]
    ar, ai, br, bi = r0 + r2, i0 + i2, r0 - r2, i0 - i2
    cr, ci, dr, di = r1 + r3, i1 + i3, r1 - r3, i1 - i3
    re = jnp.concatenate([ar + cr, br - di, ar - cr, br + di], 0)
    im = jnp.concatenate([ai + ci, bi + dr, ai - ci, bi - dr], 0)
    a, b = columns_of(re, im)
    p, q = right_dot(a, right[2]), right_dot(b, right[3])
    return planes_of(p + q, p - q)


def times(ar, ai, br, bi):
    return ar * br - ai * bi, ar * bi + ai * br


def conj_times(ar, ai, br, bi):
    return ar * br + ai * bi, ar * bi - ai * br


def by_phase(spectrum, cosine, sine):
    q = spectrum[0].shape[0] // 2
    out = []
    for i, x in enumerate(spectrum):
        at = slice(i * q, (i + 1) * q)
        out.append(jnp.concatenate(times(x[:q], x[q:], cosine[at], sine[at]), 0))
    return out


def by_residual(spectrum, observed):
    q = spectrum[0].shape[0] // 2
    out = []
    for i, x in enumerate(spectrum):
        re, im = x[:q], x[q:]
        residual = re * re + im * im - observed[i * q : (i + 1) * q]
        out.append(jnp.concatenate([residual * re, residual * im], 0))
    return out


def prepare(prop_phase, *patterns):
    n = prop_phase.shape[0]

    def kernel(phase, *refs):
        observed, outs, (held, sem) = refs[: len(patterns)], refs[len(patterns) : -2], refs[-2:]
        row = lax.broadcasted_iota(jnp.int32, (n, n), 0)
        column = lax.broadcasted_iota(jnp.int32, (n, n), 1)
        from_row = row % (n // 4) * 4 + row // (n // 4)
        from_column = column % (n // 2) * 2 + column // (n // 2)
        left = jnp.where(column == from_row, 1.0, 0.0).astype(bf16)
        right = jnp.where(row == from_column, 1.0, 0.0).astype(bf16)

        def reorder(x):
            for side in (0, 1):
                total = None
                for _ in range(3):
                    part = x.astype(bf16)
                    x = x - part.astype(f32)
                    pair = (left, part) if side == 0 else (part, right)
                    moved = jnp.dot(*pair, preferred_element_type=f32)
                    total = moved if total is None else total + moved
                x = total
            return x

        angle = reorder(phase[...])
        copies = [pltpu.make_async_copy(held.at[i], out, sem.at[i]) for i, out in enumerate(outs)]
        values = [lambda: jnp.cos(angle), lambda: jnp.sin(angle)] + [lambda x=x: reorder(x[0]) for x in observed]
        for i, value in enumerate(values):
            held[i] = value()
            copies[i].start()
        for copy in copies:
            copy.wait()

    count = 2 + len(patterns)
    return pl.pallas_call(
        kernel,
        out_shape=[pltpu.HBM((n, n), f32)] * count,
        in_specs=[VMEM] * (1 + len(patterns)),
        out_specs=[ANY] * count,
        scratch_shapes=[pltpu.VMEM((count, n, n), f32), pltpu.SemaphoreType.DMA((count,))],
        compiler_params=PARAMS,
        cost_estimate=pl.CostEstimate(flops=36 * n**3, bytes_accessed=30 * n * n, transcendentals=2 * n * n),
    )(prop_phase, *patterns)


def run_forward(s, before, patch, after, cosine, sine, tables, ready=None):
    re, im = times(before[0], before[1], patch[0], patch[1])
    spectrum = forward(re, im, tables)
    if ready is not None:
        ready()
    spectrum = by_phase(spectrum, cosine[...], sine[...])
    re, im = inverse(spectrum, tables)
    after[0] = re
    after[1] = im


def start_chunks(sources, patch, slot, sem):
    top = 0
    for source in sources:
        rows = source.shape[1]
        pltpu.make_async_copy(source, patch.at[slot, :, pl.ds(top, rows), :], sem).start()
        top += rows


def wait_slot(patch, slot, sem):
    pltpu.make_async_copy(patch.at[slot], patch.at[slot], sem).wait()


def fetch_patches(me, sources, patch, sems, which):
    for i in which:
        start_chunks(sources[i], patch, me ^ i, sems.at[me ^ i])


def grouped(refs, patches, chunks):
    return [refs[i * chunks : (i + 1) * chunks] for i in range(patches)], refs[patches * chunks :]


def early_waves(cut, patches, probe, cosine, sine, tables):
    n = probe.shape[1]
    chunks = len(patches[0])

    def kernel(cut_ref, *refs):
        sources, rest = grouped(refs, 2, chunks)
        probe, cosine, sine, right, left, waves, patch, first, phase, sems, phase_sem = rest
        me = cut_ref[0]
        pairs = ((probe, first), (cosine, phase.at[0]), (sine, phase.at[1]))
        copies = [pltpu.make_async_copy(x, y, phase_sem.at[i]) for i, (x, y) in enumerate(pairs)]

        @pl.when(me < 2)
        def _():
            fetch_patches(me, sources, patch, sems, (0, 1))
            for copy in copies:
                copy.start()
            before = first
            for s in range(2):
                wait_slot(patch, s, sems.at[s])
                if s == 0:
                    for copy in copies:
                        copy.wait()
                run_forward(s, before, patch.at[s], waves.at[s], phase.at[0], phase.at[1], (right, left))
                before = waves.at[s]

    return pl.pallas_call(
        kernel,
        out_shape=jax.ShapeDtypeStruct((2, 2, n, n), f32),
        in_specs=[SMEM] + [ANY] * (2 * chunks + 3) + [VMEM] * 2,
        out_specs=VMEM,
        scratch_shapes=[
            pltpu.VMEM((2, 2, n, n), f32),
            pltpu.VMEM((2, n, n), f32),
            pltpu.VMEM((2, n, n), f32),
            pltpu.SemaphoreType.DMA((2,)),
            pltpu.SemaphoreType.DMA((3,)),
        ],
        compiler_params=PARAMS,
        cost_estimate=SHORT,
    )(cut, *flatten(patches[:2]), *map(pinned, (probe, cosine, sine)), *tables)


def flatten(patches):
    return [chunk for patch in patches for chunk in patch]


def chain(cut, patches, early, probe, cosine, sine, observed, tables):
    n = probe.shape[1]
    sections = len(patches)
    chunks = len(patches[0])
    planes_in = [cosine, sine, observed, probe, early]

    def kernel(cut_ref, *refs):
        sources, rest = grouped(refs, sections, chunks)
        *planes, right, left, out_re, out_im, patch, waves, held, probe, sems, early_sem, held_sem = rest
        me = cut_ref[0]
        tables = (right, left)
        targets = [held.at[0], held.at[1], held.at[2], probe]
        copies = [pltpu.make_async_copy(x, y, held_sem.at[i]) for i, (x, y) in enumerate(zip(planes, targets))]
        cosine, sine, observed = [held.at[i] for i in range(3)]

        def wave(s):
            return probe if s == 0 else waves.at[s - 1]

        def back(s, re, im):
            @pl.when(me == s)
            def _():
                out_re[...], out_im[...] = conj_times(wave(s)[0], wave(s)[1], re, im)

            if s > 0:

                @pl.when(me < s)
                def _():
                    gr, gi = conj_times(patch[s, 0], patch[s, 1], re, im)
                    spectrum = by_phase(forward(gr, gi, tables), cosine[...], -sine[...])
                    back(s - 1, *inverse(spectrum, tables))

        early_copies = [pltpu.make_async_copy(planes[4].at[s], waves.at[s], early_sem.at[s]) for s in range(2)]
        for odd in range(2):

            @pl.when(me % 2 == odd)
            def _(odd=odd):
                fetch_patches(me, sources, patch, sems, (2 + odd,))

        @pl.when(me < 2)
        def _():
            early_copies[1].start()

        for i in (3, 0, 1, 2):
            copies[i].start()
        for odd in range(2):

            @pl.when(me % 2 == odd)
            def _(odd=odd):
                fetch_patches(me, sources, patch, sems, (3 - odd,))

        fetch_patches(me, sources, patch, sems, (0, 1))

        def wait_phase():
            for copy in copies[:2]:
                copy.wait()

        @pl.when(me < 2)
        def _():
            early_copies[0].start()
            early_copies[1].wait()

        @pl.when(me >= 2)
        def _():
            copies[3].wait()
            for s in range(2):
                wait_slot(patch, s, sems.at[s])
                ready = wait_phase if s == 0 else None
                run_forward(s, wave(s), patch.at[s], waves.at[s], cosine, sine, tables, ready)

        for s in range(2, sections):
            wait_slot(patch, s, sems.at[s])
            if s < sections - 1:
                ready = (lambda: pl.when(me < 2)(wait_phase)) if s == 2 else None
                run_forward(s, wave(s), patch.at[s], waves.at[s], cosine, sine, tables, ready)
        copies[2].wait()

        @pl.when(me < 2)
        def _():
            copies[3].wait()
            early_copies[0].wait()
            for s in range(2):
                wait_slot(patch, s, sems.at[s])

        last = sections - 1
        re, im = times(wave(last)[0], wave(last)[1], patch[last, 0], patch[last, 1])
        spectrum = by_residual(forward(re, im, tables), observed[...])
        back(last, *inverse(spectrum, tables))

    return pl.pallas_call(
        kernel,
        out_shape=[jax.ShapeDtypeStruct((n, n), f32)] * 2,
        in_specs=[SMEM] + [ANY] * (sections * chunks + len(planes_in)) + [VMEM] * 2,
        out_specs=[VMEM] * 2,
        scratch_shapes=[
            pltpu.VMEM((sections, 2, n, n), f32),
            pltpu.VMEM((sections - 1, 2, n, n), f32),
            pltpu.VMEM((3, n, n), f32),
            pltpu.VMEM((2, n, n), f32),
            pltpu.SemaphoreType.DMA((sections,)),
            pltpu.SemaphoreType.DMA((2,)),
            pltpu.SemaphoreType.DMA((4,)),
        ],
        compiler_params=PARAMS,
        cost_estimate=pl.CostEstimate(flops=10 * 24 * n**3, bytes_accessed=16 * n * n, transcendentals=0),
    )(cut, *flatten(patches), *map(pinned, (cosine, sine, observed, probe)), early, *tables)


def window_start(column, width, columns):
    start = jnp.minimum(column // LANE * LANE, columns - width - LANE)
    return pl.multiple_of(start, LANE), column - start


def staged(strip):
    def kernel(strip, out, sem):
        copy = pltpu.make_async_copy(strip, out, sem)
        copy.start()
        copy.wait()

    return pl.pallas_call(
        kernel,
        out_shape=pltpu.VMEM(strip.shape, f32),
        in_specs=[ANY],
        out_specs=VMEM,
        scratch_shapes=[pltpu.SemaphoreType.DMA],
        compiler_params=PARAMS,
    )(pinned(strip))


def cut_window(offsets, strip, width, bounds):
    _, _, rows, columns = strip.shape
    chunks = len(bounds) - 1

    def kernel(offsets, strip, *outs):
        row, column = offsets[0], offsets[1]
        start, shift = window_start(column, width, columns)
        for c in range(2):
            x = strip[0, c, :, pl.ds(start, width + LANE)]
            x = pltpu.roll(x, lax.rem(width + LANE - shift, width + LANE), 1)[:, :width]
            x = pltpu.roll(x, lax.rem(rows - row, rows), 0)
            for j in range(chunks):
                outs[j][c] = x[bounds[j] : bounds[j + 1]]

    return pl.pallas_call(
        kernel,
        out_shape=[jax.ShapeDtypeStruct((2, bounds[j + 1] - bounds[j], width), f32) for j in range(chunks)],
        in_specs=[SMEM, VMEM],
        out_specs=[VMEM] * chunks,
        compiler_params=PARAMS,
    )(offsets, strip)


def moved(piece, row, shift, keep):
    rows = piece.shape[0]
    x = jnp.where(keep, pltpu.roll(piece, row, 0), 0.0)
    return pltpu.roll(jnp.concatenate([x, jnp.zeros((rows, LANE), f32)], 1), shift, 1)


def place_own(offsets, came_offsets, planes, columns):
    rows, width = planes[0].shape

    def kernel(offsets, came_offsets, re, im, out, *runs):
        index = lax.broadcasted_iota(jnp.int32, (rows, width), 0)
        out[...] = jnp.zeros_like(out)
        row = offsets[0]
        start, shift = window_start(offsets[1], width, columns)
        came_start, _ = window_start(came_offsets[1], width, columns)
        for c, plane in enumerate((re, im)):
            out[0, c, :, pl.ds(start, width + LANE)] = moved(plane[...], row, shift, index >= row)
            runs[c][...] = out[0, c, :, pl.ds(came_start, width + LANE)]

    return pl.pallas_call(
        kernel,
        out_shape=[jax.ShapeDtypeStruct((1, 2, rows, columns), f32)] + [pltpu.VMEM((rows, width + LANE), f32)] * 2,
        in_specs=[SMEM, SMEM, VMEM, VMEM],
        out_specs=[VMEM] * 3,
        compiler_params=PARAMS,
    )(offsets, came_offsets, *planes)


def add_came(offsets, came, run, base, c):
    rows, width = came.shape
    columns = base.shape[3]

    def kernel(offsets, came, run, base, out, wide, sem):
        row = offsets[0]
        start, shift = window_start(offsets[1], width, columns)
        index = lax.broadcasted_iota(jnp.int32, (rows, width), 0)
        wide[...] = run[...] + moved(came[...], row, shift, index < row)
        write = pltpu.make_async_copy(wide, out.at[0, c, :, pl.ds(start, width + LANE)], sem)
        write.start()
        write.wait()

    return pl.pallas_call(
        kernel,
        out_shape=jax.ShapeDtypeStruct(base.shape, f32),
        in_specs=[SMEM, VMEM, VMEM, ANY],
        out_specs=ANY,
        input_output_aliases={3: 0},
        scratch_shapes=[pltpu.VMEM((rows, width + LANE), f32), pltpu.SemaphoreType.DMA],
        compiler_params=PARAMS,
    )(offsets, came, run, pinned(base))


def shifted(value, by):
    devices = lax.axis_size("tile")
    pairs = [(i, i + by) for i in range(devices) if 0 <= i + by < devices]
    return lax.ppermute(value, "tile", pairs)


def swapped(value, bit):
    devices = lax.axis_size("cuts")
    return lax.ppermute(value, "cuts", [(i, i ^ bit) for i in range(devices)])


def after(*values):
    return lax.optimization_barrier(values)


def merged(first, second, top, row, rows):
    index = lax.broadcasted_iota(jnp.int32, first.shape, 1) + top
    return jnp.where(index < rows - row, first, second)


BOUNDS = (0, 144, 256)


def per_device(transmission, probe, prop_phase, row_off, col_off, measured):
    rows, columns = transmission.shape[2:]
    width = probe.shape[1]
    cut = lax.axis_index("cuts").astype(jnp.int32).reshape(1)
    offsets = jnp.concatenate([row_off, col_off])
    strip = staged(transmission)
    came_offsets = shifted(offsets, 1)
    cosine, sine, observed = prepare(prop_phase, measured)
    bands = list(cut_window(came_offsets, strip, width, BOUNDS))
    below = [shifted(band, -1) for band in bands]
    own = cut_window(offsets, strip, width, BOUNDS)
    tables = [jnp.asarray(t) for t in dft_tables(width)]

    chunks, across = [], []
    below[0], cosine, sine, observed = after(below[0], cosine, sine, observed)
    for j, (first, second) in enumerate(zip(own, below)):
        if chunks:
            first, second, chunks[-1] = after(first, second, chunks[-1])
        chunks.append(merged(first, second, BOUNDS[j], row_off[0], rows))
        chunk = chunks[-1]
        across.append(swapped(chunk, 2))
    beside = [swapped(chunk, 1) for chunk in chunks]
    across[0], beside[0] = after(across[0], beside[0])
    early = early_waves(cut, [chunks, beside], probe, cosine, sine, tables)
    across[1], early = after(across[1], early)
    opposite = [swapped(chunk, 1) for chunk in across]
    planes = chain(cut, [chunks, beside, across, opposite], early, probe, cosine, sine, observed, tables)

    came = [shifted(plane, 1) for plane in planes]
    gradient, *runs = place_own(offsets, came_offsets, planes, columns)
    for c in range(2):
        gradient = add_came(came_offsets, came[c], runs[c], gradient, c)
    return gradient


def solution(mesh):
    placed = (P("cuts", None, "tile", None), P(), P(), P("tile"), P("tile"), P("tile", None, None))
    return jax.shard_map(
        per_device,
        mesh=mesh,
        in_specs=placed,
        out_specs=P("cuts", None, "tile", None),
        check_vma=False,
    )
```

```python
import jax
import jax.numpy as jnp
import numpy as np
from jax import lax
from jax.experimental import pallas as pl
from jax.experimental.pallas import tpu as pltpu
from jax.sharding import PartitionSpec as P

f32, bf16 = jnp.float32, jnp.bfloat16
LANE = 128
VMEM = pl.BlockSpec(memory_space=pltpu.VMEM)
SMEM = pl.BlockSpec(memory_space=pltpu.SMEM)
ANY = pl.BlockSpec(memory_space=pl.ANY)
SHORT = pl.CostEstimate(flops=1 << 16, bytes_accessed=1 << 12, transcendentals=0)
PARAMS = pltpu.CompilerParams(vmem_limit_bytes=12 << 20)


def dft_tables(n):
    def real_form(radix, first):
        k = np.arange(n // radix)[:, None]
        m = np.arange(n // radix)[None, :]
        angle = -2 * np.pi * ((k * (radix * m + first)) % n) / n
        c, s = np.cos(angle) / np.sqrt(n), np.sin(angle) / np.sqrt(n)
        return np.block([[c, s], [-s, c]])

    def parts(matrix):
        high = matrix.astype(np.float32).astype(jnp.bfloat16)
        low = (matrix - high.astype(np.float64)).astype(np.float32).astype(jnp.bfloat16)
        return high, low

    def for_right(matrix):
        high, low = parts(matrix)
        return np.concatenate([high, high, low], axis=0)

    def for_left(matrix):
        high, low = parts(matrix)
        return np.block([[high, high], [low, np.zeros_like(low)]])

    halves = [real_form(2, first) for first in range(2)]
    quarters = [real_form(4, first) for first in range(4)]
    right = np.stack([for_right(m) for m in halves + [m.T for m in halves]])
    left = np.stack([for_left(m) for m in [m.T for m in quarters] + quarters])
    return right, left


def pinned(x):
    return pltpu.with_memory_space_constraint(x, pltpu.HBM)


def split(x):
    high = x.astype(bf16)
    return high, (x - high.astype(f32)).astype(bf16)


def right_dot(x, table):
    high, low = split(x)
    return jnp.dot(jnp.concatenate([high, low, high], 1), table, preferred_element_type=f32)


def left_dot(table, x):
    both = jnp.dot(table, jnp.concatenate(split(x), 0), preferred_element_type=f32)
    h = both.shape[0] // 2
    return both[:h] + both[h:]


def columns_of(re, im):
    h = re.shape[1] // 2
    return (
        jnp.concatenate([re[:, :h], im[:, :h]], 1),
        jnp.concatenate([re[:, h:], im[:, h:]], 1),
    )


def planes_of(a, b):
    h = a.shape[1] // 2
    return (
        jnp.concatenate([a[:, :h], b[:, :h]], 1),
        jnp.concatenate([a[:, h:], b[:, h:]], 1),
    )


def forward(re, im, tables):
    right, left = tables
    a, b = columns_of(re, im)
    re, im = planes_of(right_dot(a + b, right[0]), right_dot(a - b, right[1]))
    q = re.shape[0] // 4
    (r0, r1, r2, r3), (i0, i1, i2, i3) = [[x[j * q : (j + 1) * q] for j in range(4)] for x in (re, im)]
    pr, pi, ur, ui = r0 + r2, i0 + i2, r0 - r2, i0 - i2
    qr, qi, vr, vi = r1 + r3, i1 + i3, r1 - r3, i1 - i3
    mixed = ((pr + qr, pi + qi), (ur + vi, ui - vr), (pr - qr, pi - qi), (ur - vi, ui + vr))
    return [left_dot(left[j], jnp.concatenate(x, 0)) for j, x in enumerate(mixed)]


def inverse(spectrum, tables):
    right, left = tables
    q = spectrum[0].shape[0] // 2
    parts = [left_dot(left[4 + j], x) for j, x in enumerate(spectrum)]
    (r0, i0), (r1, i1), (r2, i2), (r3, i3) = [(x[:q], x[q:]) for x in parts]
    ar, ai, br, bi = r0 + r2, i0 + i2, r0 - r2, i0 - i2
    cr, ci, dr, di = r1 + r3, i1 + i3, r1 - r3, i1 - i3
    re = jnp.concatenate([ar + cr, br - di, ar - cr, br + di], 0)
    im = jnp.concatenate([ai + ci, bi + dr, ai - ci, bi - dr], 0)
    a, b = columns_of(re, im)
    p, q = right_dot(a, right[2]), right_dot(b, right[3])
    return planes_of(p + q, p - q)


def times(ar, ai, br, bi):
    return ar * br - ai * bi, ar * bi + ai * br


def conj_times(ar, ai, br, bi):
    return ar * br + ai * bi, ar * bi - ai * br


def by_phase(spectrum, cosine, sine, product=times):
    q = spectrum[0].shape[0] // 2
    out = []
    for i, x in enumerate(spectrum):
        at = slice(i * q, (i + 1) * q)
        out.append(jnp.concatenate(product(cosine[at], sine[at], x[:q], x[q:]), 0))
    return out


def by_residual(spectrum, observed):
    q = spectrum[0].shape[0] // 2
    out = []
    for i, x in enumerate(spectrum):
        re, im = x[:q], x[q:]
        residual = re * re + im * im - observed[i * q : (i + 1) * q]
        out.append(jnp.concatenate([residual * re, residual * im], 0))
    return out


def prepare(prop_phase, *patterns):
    n = prop_phase.shape[0]

    def kernel(phase, *refs):
        observed, outs, (held, sem) = refs[: len(patterns)], refs[len(patterns) : -2], refs[-2:]
        row = lax.broadcasted_iota(jnp.int32, (n, n), 0)
        column = lax.broadcasted_iota(jnp.int32, (n, n), 1)
        from_row = row % (n // 4) * 4 + row // (n // 4)
        from_column = column % (n // 2) * 2 + column // (n // 2)
        left = jnp.where(column == from_row, 1.0, 0.0).astype(bf16)
        right = jnp.where(row == from_column, 1.0, 0.0).astype(bf16)

        def reorder(x):
            for side in (0, 1):
                total = None
                for _ in range(3):
                    part = x.astype(bf16)
                    x = x - part.astype(f32)
                    pair = (left, part) if side == 0 else (part, right)
                    moved = jnp.dot(*pair, preferred_element_type=f32)
                    total = moved if total is None else total + moved
                x = total
            return x

        angle = reorder(phase[...])
        copies = [pltpu.make_async_copy(held.at[i], out, sem.at[i]) for i, out in enumerate(outs)]
        values = [lambda: jnp.cos(angle), lambda: jnp.sin(angle)] + [lambda x=x: reorder(x[0]) for x in observed]
        for i, value in enumerate(values):
            held[i] = value()
            copies[i].start()
        for copy in copies:
            copy.wait()

    count = 2 + len(patterns)
    return pl.pallas_call(
        kernel,
        out_shape=[pltpu.HBM((n, n), f32)] * count,
        in_specs=[VMEM] * (1 + len(patterns)),
        out_specs=[ANY] * count,
        scratch_shapes=[pltpu.VMEM((count, n, n), f32), pltpu.SemaphoreType.DMA((count,))],
        compiler_params=PARAMS,
        cost_estimate=pl.CostEstimate(flops=36 * n**3, bytes_accessed=30 * n * n, transcendentals=2 * n * n),
    )(prop_phase, *patterns)


def run_forward(s, before, patch, after, cosine, sine, tables, ready=None):
    re, im = times(before[0], before[1], patch[0], patch[1])
    spectrum = forward(re, im, tables)
    if ready is not None:
        ready()
    spectrum = by_phase(spectrum, cosine[...], sine[...])
    re, im = inverse(spectrum, tables)
    after[0] = re
    after[1] = im


def start_chunks(sources, patch, slot, sem):
    top = 0
    for source in sources:
        rows = source.shape[1]
        pltpu.make_async_copy(source, patch.at[slot, :, pl.ds(top, rows), :], sem).start()
        top += rows


def wait_slot(patch, slot, sem):
    pltpu.make_async_copy(patch.at[slot], patch.at[slot], sem).wait()


def fetch_patches(me, sources, patch, sems, which):
    for i in which:
        start_chunks(sources[i], patch, me ^ i, sems.at[me ^ i])


def grouped(refs, patches, chunks):
    return [refs[i * chunks : (i + 1) * chunks] for i in range(patches)], refs[patches * chunks :]


def early_waves(cut, patches, probe, cosine, sine, tables):
    n = probe.shape[1]
    chunks = len(patches[0])

    def kernel(cut_ref, *refs):
        sources, rest = grouped(refs, 2, chunks)
        probe, cosine, sine, right, left, waves, patch, first, phase, sems, phase_sem = rest
        me = cut_ref[0]
        pairs = ((probe, first), (cosine, phase.at[0]), (sine, phase.at[1]))
        copies = [pltpu.make_async_copy(x, y, phase_sem.at[i]) for i, (x, y) in enumerate(pairs)]

        @pl.when(me < 2)
        def _():
            fetch_patches(me, sources, patch, sems, (0, 1))
            for copy in copies:
                copy.start()
            before = first
            for s in range(2):
                wait_slot(patch, s, sems.at[s])
                if s == 0:
                    for copy in copies:
                        copy.wait()
                run_forward(s, before, patch.at[s], waves.at[s], phase.at[0], phase.at[1], (right, left))
                before = waves.at[s]

    return pl.pallas_call(
        kernel,
        out_shape=jax.ShapeDtypeStruct((2, 2, n, n), f32),
        in_specs=[SMEM] + [ANY] * (2 * chunks + 3) + [VMEM] * 2,
        out_specs=VMEM,
        scratch_shapes=[
            pltpu.VMEM((2, 2, n, n), f32),
            pltpu.VMEM((2, n, n), f32),
            pltpu.VMEM((2, n, n), f32),
            pltpu.SemaphoreType.DMA((2,)),
            pltpu.SemaphoreType.DMA((3,)),
        ],
        compiler_params=PARAMS,
        cost_estimate=SHORT,
    )(cut, *flatten(patches[:2]), *map(pinned, (probe, cosine, sine)), *tables)


def flatten(patches):
    return [chunk for patch in patches for chunk in patch]


def chain(cut, patches, early, probe, cosine, sine, observed, tables):
    n = probe.shape[1]
    sections = len(patches)
    chunks = len(patches[0])
    planes_in = [cosine, sine, observed, probe, early]

    def kernel(cut_ref, *refs):
        sources, rest = grouped(refs, sections, chunks)
        *planes, right, left, out_re, out_im, patch, waves, held, probe, sems, early_sem, held_sem = rest
        me = cut_ref[0]
        tables = (right, left)
        targets = [held.at[0], held.at[1], held.at[2], probe]
        copies = [pltpu.make_async_copy(x, y, held_sem.at[i]) for i, (x, y) in enumerate(zip(planes, targets))]
        cosine, sine, observed = [held.at[i] for i in range(3)]

        def wave(s):
            return probe if s == 0 else waves.at[s - 1]

        def back(s, re, im):
            @pl.when(me == s)
            def _():
                out_re[...], out_im[...] = conj_times(wave(s)[0], wave(s)[1], re, im)

            if s > 0:

                @pl.when(me < s)
                def _():
                    gr, gi = conj_times(patch[s, 0], patch[s, 1], re, im)
                    spectrum = by_phase(forward(gr, gi, tables), cosine[...], sine[...], conj_times)
                    back(s - 1, *inverse(spectrum, tables))

        early_copies = [pltpu.make_async_copy(planes[4].at[s], waves.at[s], early_sem.at[s]) for s in range(2)]
        for odd in range(2):

            @pl.when(me % 2 == odd)
            def _(odd=odd):
                fetch_patches(me, sources, patch, sems, (2 + odd,))

        @pl.when(me < 2)
        def _():
            early_copies[1].start()

        for i in (3, 0, 1, 2):
            copies[i].start()
        for odd in range(2):

            @pl.when(me % 2 == odd)
            def _(odd=odd):
                fetch_patches(me, sources, patch, sems, (3 - odd,))

        fetch_patches(me, sources, patch, sems, (0, 1))

        def wait_phase():
            for copy in copies[:2]:
                copy.wait()

        @pl.when(me < 2)
        def _():
            early_copies[0].start()
            early_copies[1].wait()

        @pl.when(me >= 2)
        def _():
            copies[3].wait()
            for s in range(2):
                wait_slot(patch, s, sems.at[s])
                ready = wait_phase if s == 0 else None
                run_forward(s, wave(s), patch.at[s], waves.at[s], cosine, sine, tables, ready)

        for s in range(2, sections):
            wait_slot(patch, s, sems.at[s])
            if s < sections - 1:
                ready = (lambda: pl.when(me < 2)(wait_phase)) if s == 2 else None
                run_forward(s, wave(s), patch.at[s], waves.at[s], cosine, sine, tables, ready)
        copies[2].wait()

        @pl.when(me < 2)
        def _():
            copies[3].wait()
            early_copies[0].wait()
            for s in range(2):
                wait_slot(patch, s, sems.at[s])

        last = sections - 1
        re, im = times(wave(last)[0], wave(last)[1], patch[last, 0], patch[last, 1])
        spectrum = by_residual(forward(re, im, tables), observed[...])
        back(last, *inverse(spectrum, tables))

    return pl.pallas_call(
        kernel,
        out_shape=[jax.ShapeDtypeStruct((n, n), f32)] * 2,
        in_specs=[SMEM] + [ANY] * (sections * chunks + len(planes_in)) + [VMEM] * 2,
        out_specs=[VMEM] * 2,
        scratch_shapes=[
            pltpu.VMEM((sections, 2, n, n), f32),
            pltpu.VMEM((sections - 1, 2, n, n), f32),
            pltpu.VMEM((3, n, n), f32),
            pltpu.VMEM((2, n, n), f32),
            pltpu.SemaphoreType.DMA((sections,)),
            pltpu.SemaphoreType.DMA((2,)),
            pltpu.SemaphoreType.DMA((4,)),
        ],
        compiler_params=PARAMS,
        cost_estimate=pl.CostEstimate(flops=10 * 24 * n**3, bytes_accessed=16 * n * n, transcendentals=0),
    )(cut, *flatten(patches), *map(pinned, (cosine, sine, observed, probe)), early, *tables)


def window_start(column, width, columns):
    start = jnp.minimum(column // LANE * LANE, columns - width - LANE)
    return pl.multiple_of(start, LANE), column - start


def staged(strip):
    def kernel(strip, out, sem):
        copy = pltpu.make_async_copy(strip, out, sem)
        copy.start()
        copy.wait()

    return pl.pallas_call(
        kernel,
        out_shape=pltpu.VMEM(strip.shape, f32),
        in_specs=[ANY],
        out_specs=VMEM,
        scratch_shapes=[pltpu.SemaphoreType.DMA],
        compiler_params=PARAMS,
    )(pinned(strip))


def cut_window(offsets, strip, width, bounds):
    _, _, rows, columns = strip.shape
    chunks = len(bounds) - 1

    def kernel(offsets, strip, *outs):
        row, column = offsets[0], offsets[1]
        start, shift = window_start(column, width, columns)
        for c in range(2):
            x = strip[0, c, :, pl.ds(start, width + LANE)]
            x = pltpu.roll(x, lax.rem(width + LANE - shift, width + LANE), 1)[:, :width]
            x = pltpu.roll(x, lax.rem(rows - row, rows), 0)
            for j in range(chunks):
                outs[j][c] = x[bounds[j] : bounds[j + 1]]

    return pl.pallas_call(
        kernel,
        out_shape=[jax.ShapeDtypeStruct((2, bounds[j + 1] - bounds[j], width), f32) for j in range(chunks)],
        in_specs=[SMEM, VMEM],
        out_specs=[VMEM] * chunks,
        compiler_params=PARAMS,
    )(offsets, strip)


def moved(piece, row, shift, keep):
    rows = piece.shape[0]
    x = jnp.where(keep, pltpu.roll(piece, row, 0), 0.0)
    return pltpu.roll(jnp.concatenate([x, jnp.zeros((rows, LANE), f32)], 1), shift, 1)


def place_own(offsets, came_offsets, planes, columns):
    rows, width = planes[0].shape

    def kernel(offsets, came_offsets, re, im, out, *runs):
        index = lax.broadcasted_iota(jnp.int32, (rows, width), 0)
        out[...] = jnp.zeros_like(out)
        row = offsets[0]
        start, shift = window_start(offsets[1], width, columns)
        came_start, _ = window_start(came_offsets[1], width, columns)
        for c, plane in enumerate((re, im)):
            out[0, c, :, pl.ds(start, width + LANE)] = moved(plane[...], row, shift, index >= row)
            runs[c][...] = out[0, c, :, pl.ds(came_start, width + LANE)]

    return pl.pallas_call(
        kernel,
        out_shape=[jax.ShapeDtypeStruct((1, 2, rows, columns), f32)] + [pltpu.VMEM((rows, width + LANE), f32)] * 2,
        in_specs=[SMEM, SMEM, VMEM, VMEM],
        out_specs=[VMEM] * 3,
        compiler_params=PARAMS,
    )(offsets, came_offsets, *planes)


def add_came(offsets, came, run, base, c):
    rows, width = came.shape
    columns = base.shape[3]

    def kernel(offsets, came, run, base, out, wide, sem):
        row = offsets[0]
        start, shift = window_start(offsets[1], width, columns)
        index = lax.broadcasted_iota(jnp.int32, (rows, width), 0)
        wide[...] = run[...] + moved(came[...], row, shift, index < row)
        write = pltpu.make_async_copy(wide, out.at[0, c, :, pl.ds(start, width + LANE)], sem)
        write.start()
        write.wait()

    return pl.pallas_call(
        kernel,
        out_shape=jax.ShapeDtypeStruct(base.shape, f32),
        in_specs=[SMEM, VMEM, VMEM, ANY],
        out_specs=ANY,
        input_output_aliases={3: 0},
        scratch_shapes=[pltpu.VMEM((rows, width + LANE), f32), pltpu.SemaphoreType.DMA],
        compiler_params=PARAMS,
    )(offsets, came, run, pinned(base))


def shifted(value, by):
    devices = lax.axis_size("tile")
    pairs = [(i, i + by) for i in range(devices) if 0 <= i + by < devices]
    return lax.ppermute(value, "tile", pairs)


def swapped(value, bit):
    devices = lax.axis_size("cuts")
    return lax.ppermute(value, "cuts", [(i, i ^ bit) for i in range(devices)])


def after(*values):
    return lax.optimization_barrier(values)


def merged(first, second, top, row, rows):
    index = lax.broadcasted_iota(jnp.int32, first.shape, 1) + top
    return jnp.where(index < rows - row, first, second)


BOUNDS = (0, 152, 256)


def per_device(transmission, probe, prop_phase, row_off, col_off, measured):
    rows, columns = transmission.shape[2:]
    width = probe.shape[1]
    cut = lax.axis_index("cuts").astype(jnp.int32).reshape(1)
    offsets = jnp.concatenate([row_off, col_off])
    strip = staged(transmission)
    came_offsets = shifted(offsets, 1)
    cosine, sine, observed = prepare(prop_phase, measured)
    bands = list(cut_window(came_offsets, strip, width, BOUNDS))
    below = [shifted(band, -1) for band in bands]
    own = cut_window(offsets, strip, width, BOUNDS)
    tables = [jnp.asarray(t) for t in dft_tables(width)]

    chunks, across = [], []
    below[0], cosine, sine, observed = after(below[0], cosine, sine, observed)
    for j, (first, second) in enumerate(zip(own, below)):
        if chunks:
            first, second, chunks[-1] = after(first, second, chunks[-1])
        chunks.append(merged(first, second, BOUNDS[j], row_off[0], rows))
        chunk = chunks[-1]
        across.append(swapped(chunk, 2))
    beside = [swapped(chunk, 1) for chunk in chunks]
    across[0], beside[0] = after(across[0], beside[0])
    early = early_waves(cut, [chunks, beside], probe, cosine, sine, tables)
    across[1], early = after(across[1], early)
    opposite = [swapped(chunk, 1) for chunk in across]
    planes = chain(cut, [chunks, beside, across, opposite], early, probe, cosine, sine, observed, tables)

    came = [shifted(plane, 1) for plane in planes]
    gradient, *runs = place_own(offsets, came_offsets, planes, columns)
    for c in range(2):
        gradient = add_came(came_offsets, came[c], runs[c], gradient, c)
    return gradient


def solution(mesh):
    placed = (P("cuts", None, "tile", None), P(), P(), P("tile"), P("tile"), P("tile", None, None))
    return jax.shard_map(
        per_device,
        mesh=mesh,
        in_specs=placed,
        out_specs=P("cuts", None, "tile", None),
        check_vma=False,
    )
```

```python
import jax
import jax.numpy as jnp
import numpy as np
from jax import lax
from jax.experimental import pallas as pl
from jax.experimental.pallas import tpu as pltpu
from jax.sharding import PartitionSpec as P

f32, bf16 = jnp.float32, jnp.bfloat16
LANE = 128
VMEM = pl.BlockSpec(memory_space=pltpu.VMEM)
SMEM = pl.BlockSpec(memory_space=pltpu.SMEM)
ANY = pl.BlockSpec(memory_space=pl.ANY)
SHORT = pl.CostEstimate(flops=1 << 16, bytes_accessed=1 << 12, transcendentals=0)
PARAMS = pltpu.CompilerParams(vmem_limit_bytes=12 << 20)


def dft_tables(n):
    def real_form(radix, first):
        k = np.arange(n // radix)[:, None]
        m = np.arange(n // radix)[None, :]
        angle = -2 * np.pi * ((k * (radix * m + first)) % n) / n
        c, s = np.cos(angle) / np.sqrt(n), np.sin(angle) / np.sqrt(n)
        return np.block([[c, s], [-s, c]])

    def parts(matrix):
        high = matrix.astype(np.float32).astype(jnp.bfloat16)
        low = (matrix - high.astype(np.float64)).astype(np.float32).astype(jnp.bfloat16)
        return high, low

    def for_right(matrix):
        high, low = parts(matrix)
        return np.concatenate([high, high, low], axis=0)

    def for_left(matrix):
        high, low = parts(matrix)
        return np.block([[high, high], [low, np.zeros_like(low)]])

    halves = [real_form(2, first) for first in range(2)]
    quarters = [real_form(4, first) for first in range(4)]
    right = np.stack([for_right(m) for m in halves + [m.T for m in halves]])
    left = np.stack([for_left(m) for m in [m.T for m in quarters] + quarters])
    return right, left


def pinned(x):
    return pltpu.with_memory_space_constraint(x, pltpu.HBM)


def split(x):
    high = x.astype(bf16)
    return high, (x - high.astype(f32)).astype(bf16)


def right_dot(x, table):
    high, low = split(x)
    return jnp.dot(jnp.concatenate([high, low, high], 1), table, preferred_element_type=f32)


def left_dot(table, x):
    both = jnp.dot(table, jnp.concatenate(split(x), 0), preferred_element_type=f32)
    h = both.shape[0] // 2
    return both[:h] + both[h:]


def columns_of(re, im):
    h = re.shape[1] // 2
    return (
        jnp.concatenate([re[:, :h], im[:, :h]], 1),
        jnp.concatenate([re[:, h:], im[:, h:]], 1),
    )


def planes_of(a, b):
    h = a.shape[1] // 2
    return (
        jnp.concatenate([a[:, :h], b[:, :h]], 1),
        jnp.concatenate([a[:, h:], b[:, h:]], 1),
    )


def forward(re, im, tables):
    right, left = tables
    a, b = columns_of(re, im)
    re, im = planes_of(right_dot(a + b, right[0]), right_dot(a - b, right[1]))
    q = re.shape[0] // 4
    (r0, r1, r2, r3), (i0, i1, i2, i3) = [[x[j * q : (j + 1) * q] for j in range(4)] for x in (re, im)]
    pr, pi, ur, ui = r0 + r2, i0 + i2, r0 - r2, i0 - i2
    qr, qi, vr, vi = r1 + r3, i1 + i3, r1 - r3, i1 - i3
    mixed = ((pr + qr, pi + qi), (ur + vi, ui - vr), (pr - qr, pi - qi), (ur - vi, ui + vr))
    return [left_dot(left[j], jnp.concatenate(x, 0)) for j, x in enumerate(mixed)]


def inverse(spectrum, tables):
    right, left = tables
    q = spectrum[0].shape[0] // 2
    parts = [left_dot(left[4 + j], x) for j, x in enumerate(spectrum)]
    (r0, i0), (r1, i1), (r2, i2), (r3, i3) = [(x[:q], x[q:]) for x in parts]
    ar, ai, br, bi = r0 + r2, i0 + i2, r0 - r2, i0 - i2
    cr, ci, dr, di = r1 + r3, i1 + i3, r1 - r3, i1 - i3
    re = jnp.concatenate([ar + cr, br - di, ar - cr, br + di], 0)
    im = jnp.concatenate([ai + ci, bi + dr, ai - ci, bi - dr], 0)
    a, b = columns_of(re, im)
    p, q = right_dot(a, right[2]), right_dot(b, right[3])
    return planes_of(p + q, p - q)


def times(ar, ai, br, bi):
    return ar * br - ai * bi, ar * bi + ai * br


def conj_times(ar, ai, br, bi):
    return ar * br + ai * bi, ar * bi - ai * br


def by_phase(spectrum, cosine, sine, product=times):
    q = spectrum[0].shape[0] // 2
    out = []
    for i, x in enumerate(spectrum):
        at = slice(i * q, (i + 1) * q)
        out.append(jnp.concatenate(product(cosine[at], sine[at], x[:q], x[q:]), 0))
    return out


def by_residual(spectrum, observed):
    q = spectrum[0].shape[0] // 2
    out = []
    for i, x in enumerate(spectrum):
        re, im = x[:q], x[q:]
        residual = re * re + im * im - observed[i * q : (i + 1) * q]
        out.append(jnp.concatenate([residual * re, residual * im], 0))
    return out


def prepare(prop_phase, *patterns):
    n = prop_phase.shape[0]

    def kernel(phase, *refs):
        observed, outs, (held, sem) = refs[: len(patterns)], refs[len(patterns) : -2], refs[-2:]
        row = lax.broadcasted_iota(jnp.int32, (n, n), 0)
        column = lax.broadcasted_iota(jnp.int32, (n, n), 1)
        from_row = row % (n // 4) * 4 + row // (n // 4)
        from_column = column % (n // 2) * 2 + column // (n // 2)
        left = jnp.where(column == from_row, 1.0, 0.0).astype(bf16)
        right = jnp.where(row == from_column, 1.0, 0.0).astype(bf16)

        def reorder(x):
            for side in (0, 1):
                total = None
                for _ in range(3):
                    part = x.astype(bf16)
                    x = x - part.astype(f32)
                    pair = (left, part) if side == 0 else (part, right)
                    moved = jnp.dot(*pair, preferred_element_type=f32)
                    total = moved if total is None else total + moved
                x = total
            return x

        angle = reorder(phase[...])
        copies = [pltpu.make_async_copy(held.at[i], out, sem.at[i]) for i, out in enumerate(outs)]
        values = [lambda: jnp.cos(angle), lambda: jnp.sin(angle)] + [lambda x=x: reorder(x[0]) for x in observed]
        for i, value in enumerate(values):
            held[i] = value()
            copies[i].start()
        for copy in copies:
            copy.wait()

    count = 2 + len(patterns)
    return pl.pallas_call(
        kernel,
        out_shape=[pltpu.HBM((n, n), f32)] * count,
        in_specs=[VMEM] * (1 + len(patterns)),
        out_specs=[ANY] * count,
        scratch_shapes=[pltpu.VMEM((count, n, n), f32), pltpu.SemaphoreType.DMA((count,))],
        compiler_params=PARAMS,
        cost_estimate=pl.CostEstimate(flops=36 * n**3, bytes_accessed=30 * n * n, transcendentals=2 * n * n),
    )(prop_phase, *patterns)


def run_forward(s, before, patch, after, cosine, sine, tables, ready=None):
    re, im = times(before[0], before[1], patch[0], patch[1])
    spectrum = forward(re, im, tables)
    if ready is not None:
        ready()
    spectrum = by_phase(spectrum, cosine[...], sine[...])
    re, im = inverse(spectrum, tables)
    after[0] = re
    after[1] = im


def start_chunks(sources, patch, slot, sem):
    top = 0
    for source in sources:
        rows = source.shape[1]
        pltpu.make_async_copy(source, patch.at[slot, :, pl.ds(top, rows), :], sem).start()
        top += rows


def wait_slot(patch, slot, sem):
    pltpu.make_async_copy(patch.at[slot], patch.at[slot], sem).wait()


def fetch_patches(me, sources, patch, sems, which):
    for i in which:
        start_chunks(sources[i], patch, me ^ i, sems.at[me ^ i])


def grouped(refs, patches, chunks):
    return [refs[i * chunks : (i + 1) * chunks] for i in range(patches)], refs[patches * chunks :]


def early_waves(cut, patches, probe, cosine, sine, tables):
    n = probe.shape[1]
    chunks = len(patches[0])

    def kernel(cut_ref, *refs):
        sources, rest = grouped(refs, 2, chunks)
        probe, cosine, sine, right, left, waves, patch, first, phase, sems, phase_sem = rest
        me = cut_ref[0]
        pairs = ((probe, first), (cosine, phase.at[0]), (sine, phase.at[1]))
        copies = [pltpu.make_async_copy(x, y, phase_sem.at[i]) for i, (x, y) in enumerate(pairs)]

        @pl.when(me < 2)
        def _():
            fetch_patches(me, sources, patch, sems, (0, 1))
            for copy in copies:
                copy.start()
            before = first
            for s in range(2):
                wait_slot(patch, s, sems.at[s])
                if s == 0:
                    for copy in copies:
                        copy.wait()
                run_forward(s, before, patch.at[s], waves.at[s], phase.at[0], phase.at[1], (right, left))
                before = waves.at[s]

    return pl.pallas_call(
        kernel,
        out_shape=jax.ShapeDtypeStruct((2, 2, n, n), f32),
        in_specs=[SMEM] + [ANY] * (2 * chunks + 3) + [VMEM] * 2,
        out_specs=VMEM,
        scratch_shapes=[
            pltpu.VMEM((2, 2, n, n), f32),
            pltpu.VMEM((2, n, n), f32),
            pltpu.VMEM((2, n, n), f32),
            pltpu.SemaphoreType.DMA((2,)),
            pltpu.SemaphoreType.DMA((3,)),
        ],
        compiler_params=PARAMS,
        cost_estimate=SHORT,
    )(cut, *flatten(patches[:2]), *map(pinned, (probe, cosine, sine)), *tables)


def flatten(patches):
    return [chunk for patch in patches for chunk in patch]


def chain(cut, patches, early, probe, cosine, sine, observed, tables):
    n = probe.shape[1]
    sections = len(patches)
    chunks = len(patches[0])
    planes_in = [cosine, sine, observed, probe, early]

    def kernel(cut_ref, *refs):
        sources, rest = grouped(refs, sections, chunks)
        *planes, right, left, out_re, out_im, patch, waves, held, probe, sems, early_sem, held_sem = rest
        me = cut_ref[0]
        tables = (right, left)
        targets = [held.at[0], held.at[1], held.at[2], probe]
        copies = [pltpu.make_async_copy(x, y, held_sem.at[i]) for i, (x, y) in enumerate(zip(planes, targets))]
        cosine, sine, observed = [held.at[i] for i in range(3)]

        def wave(s):
            return probe if s == 0 else waves.at[s - 1]

        def back(s, re, im):
            @pl.when(me == s)
            def _():
                out_re[...], out_im[...] = conj_times(wave(s)[0], wave(s)[1], re, im)

            if s > 0:

                @pl.when(me < s)
                def _():
                    gr, gi = conj_times(patch[s, 0], patch[s, 1], re, im)
                    spectrum = by_phase(forward(gr, gi, tables), cosine[...], sine[...], conj_times)
                    back(s - 1, *inverse(spectrum, tables))

        early_copies = [pltpu.make_async_copy(planes[4].at[s], waves.at[s], early_sem.at[s]) for s in range(2)]
        for odd in range(2):

            @pl.when(me % 2 == odd)
            def _(odd=odd):
                fetch_patches(me, sources, patch, sems, (2 + odd,))

        @pl.when(me < 2)
        def _():
            early_copies[1].start()

        for i in (3, 0, 1, 2):
            copies[i].start()
        for odd in range(2):

            @pl.when(me % 2 == odd)
            def _(odd=odd):
                fetch_patches(me, sources, patch, sems, (3 - odd,))

        fetch_patches(me, sources, patch, sems, (0, 1))

        def wait_phase():
            for copy in copies[:2]:
                copy.wait()

        @pl.when(me < 2)
        def _():
            early_copies[0].start()
            early_copies[1].wait()

        @pl.when(me >= 2)
        def _():
            copies[3].wait()
            for s in range(2):
                wait_slot(patch, s, sems.at[s])
                ready = wait_phase if s == 0 else None
                run_forward(s, wave(s), patch.at[s], waves.at[s], cosine, sine, tables, ready)

        for s in range(2, sections):
            wait_slot(patch, s, sems.at[s])
            if s < sections - 1:
                ready = (lambda: pl.when(me < 2)(wait_phase)) if s == 2 else None
                run_forward(s, wave(s), patch.at[s], waves.at[s], cosine, sine, tables, ready)
        copies[2].wait()

        @pl.when(me < 2)
        def _():
            copies[3].wait()
            early_copies[0].wait()
            for s in range(2):
                wait_slot(patch, s, sems.at[s])

        last = sections - 1
        re, im = times(wave(last)[0], wave(last)[1], patch[last, 0], patch[last, 1])
        spectrum = by_residual(forward(re, im, tables), observed[...])
        back(last, *inverse(spectrum, tables))

    return pl.pallas_call(
        kernel,
        out_shape=[jax.ShapeDtypeStruct((n, n), f32)] * 2,
        in_specs=[SMEM] + [ANY] * (sections * chunks + len(planes_in)) + [VMEM] * 2,
        out_specs=[VMEM] * 2,
        scratch_shapes=[
            pltpu.VMEM((sections, 2, n, n), f32),
            pltpu.VMEM((sections - 1, 2, n, n), f32),
            pltpu.VMEM((3, n, n), f32),
            pltpu.VMEM((2, n, n), f32),
            pltpu.SemaphoreType.DMA((sections,)),
            pltpu.SemaphoreType.DMA((2,)),
            pltpu.SemaphoreType.DMA((4,)),
        ],
        compiler_params=PARAMS,
        cost_estimate=pl.CostEstimate(flops=10 * 24 * n**3, bytes_accessed=16 * n * n, transcendentals=0),
    )(cut, *flatten(patches), *map(pinned, (cosine, sine, observed, probe)), early, *tables)


def window_start(column, width, columns):
    start = jnp.minimum(column // LANE * LANE, columns - width - LANE)
    return pl.multiple_of(start, LANE), column - start


def staged(strip):
    def kernel(strip, out, sem):
        copy = pltpu.make_async_copy(strip, out, sem)
        copy.start()
        copy.wait()

    return pl.pallas_call(
        kernel,
        out_shape=pltpu.VMEM(strip.shape, f32),
        in_specs=[ANY],
        out_specs=VMEM,
        scratch_shapes=[pltpu.SemaphoreType.DMA],
        compiler_params=PARAMS,
    )(pinned(strip))


def cut_window(offsets, strip, width, bounds):
    _, _, rows, columns = strip.shape
    chunks = len(bounds) - 1

    def kernel(offsets, strip, *outs):
        row, column = offsets[0], offsets[1]
        start, shift = window_start(column, width, columns)
        for c in range(2):
            x = strip[0, c, :, pl.ds(start, width + LANE)]
            x = pltpu.roll(x, lax.rem(width + LANE - shift, width + LANE), 1)[:, :width]
            x = pltpu.roll(x, lax.rem(rows - row, rows), 0)
            for j in range(chunks):
                outs[j][c] = x[bounds[j] : bounds[j + 1]]

    return pl.pallas_call(
        kernel,
        out_shape=[jax.ShapeDtypeStruct((2, bounds[j + 1] - bounds[j], width), f32) for j in range(chunks)],
        in_specs=[SMEM, VMEM],
        out_specs=[VMEM] * chunks,
        compiler_params=PARAMS,
    )(offsets, strip)


def moved(piece, row, shift, keep):
    return shifted_right(jnp.where(keep, pltpu.roll(piece, row, 0), 0.0), shift)


def shifted_right(x, shift):
    return pltpu.roll(jnp.concatenate([x, jnp.zeros((x.shape[0], LANE), f32)], 1), shift, 1)


def place_own(offsets, came_offsets, planes, columns):
    rows, width = planes[0].shape

    def kernel(offsets, came_offsets, re, im, out, *runs):
        index = lax.broadcasted_iota(jnp.int32, (rows, width), 0)
        out[...] = jnp.zeros_like(out)
        row = offsets[0]
        start, shift = window_start(offsets[1], width, columns)
        came_start, _ = window_start(came_offsets[1], width, columns)
        for c, plane in enumerate((re, im)):
            out[0, c, :, pl.ds(start, width + LANE)] = moved(plane[...], row, shift, index >= row)
            runs[c][...] = out[0, c, :, pl.ds(came_start, width + LANE)]

    return pl.pallas_call(
        kernel,
        out_shape=[jax.ShapeDtypeStruct((1, 2, rows, columns), f32)] + [pltpu.VMEM((rows, width + LANE), f32)] * 2,
        in_specs=[SMEM, SMEM, VMEM, VMEM],
        out_specs=[VMEM] * 3,
        compiler_params=PARAMS,
    )(offsets, came_offsets, *planes)


def add_came(offsets, came, run, base, c):
    rows, width = came.shape
    columns = base.shape[3]

    parts = 4
    step = rows // parts

    def kernel(offsets, came, run, base, out, wide, sem):
        row = offsets[0]
        start, shift = window_start(offsets[1], width, columns)
        index = lax.broadcasted_iota(jnp.int32, (rows, width), 0)
        x = jnp.where(index < row, pltpu.roll(came[...], row, 0), 0.0)
        writes = []
        for part in range(parts):
            at = pl.ds(part * step, step)
            wide[at] = run[at] + shifted_right(x[part * step : (part + 1) * step], shift)
            to = out.at[0, c, at, pl.ds(start, width + LANE)]
            writes.append(pltpu.make_async_copy(wide.at[at], to, sem.at[part]))
            writes[-1].start()
        for write in writes:
            write.wait()

    return pl.pallas_call(
        kernel,
        out_shape=jax.ShapeDtypeStruct(base.shape, f32),
        in_specs=[SMEM, VMEM, VMEM, ANY],
        out_specs=ANY,
        input_output_aliases={3: 0},
        scratch_shapes=[pltpu.VMEM((rows, width + LANE), f32), pltpu.SemaphoreType.DMA((parts,))],
        compiler_params=PARAMS,
    )(offsets, came, run, pinned(base))


def shifted(value, by):
    devices = lax.axis_size("tile")
    pairs = [(i, i + by) for i in range(devices) if 0 <= i + by < devices]
    return lax.ppermute(value, "tile", pairs)


def swapped(value, bit):
    devices = lax.axis_size("cuts")
    return lax.ppermute(value, "cuts", [(i, i ^ bit) for i in range(devices)])


def after(*values):
    return lax.optimization_barrier(values)


def merged(first, second, top, row, rows):
    index = lax.broadcasted_iota(jnp.int32, first.shape, 1) + top
    return jnp.where(index < rows - row, first, second)


BOUNDS = (0, 152, 256)


def per_device(transmission, probe, prop_phase, row_off, col_off, measured):
    rows, columns = transmission.shape[2:]
    width = probe.shape[1]
    cut = lax.axis_index("cuts").astype(jnp.int32).reshape(1)
    offsets = jnp.concatenate([row_off, col_off])
    strip = staged(transmission)
    came_offsets = shifted(offsets, 1)
    cosine, sine, observed = prepare(prop_phase, measured)
    bands = list(cut_window(came_offsets, strip, width, BOUNDS))
    below = [shifted(band, -1) for band in bands]
    own = cut_window(offsets, strip, width, BOUNDS)
    tables = [jnp.asarray(t) for t in dft_tables(width)]

    chunks, across = [], []
    below[0], cosine, sine, observed = after(below[0], cosine, sine, observed)
    for j, (first, second) in enumerate(zip(own, below)):
        if chunks:
            first, second, chunks[-1] = after(first, second, chunks[-1])
        chunks.append(merged(first, second, BOUNDS[j], row_off[0], rows))
        chunk = chunks[-1]
        across.append(swapped(chunk, 2))
    beside = [swapped(chunk, 1) for chunk in chunks]
    across[0], beside[0] = after(across[0], beside[0])
    early = early_waves(cut, [chunks, beside], probe, cosine, sine, tables)
    across[1], early = after(across[1], early)
    opposite = [swapped(chunk, 1) for chunk in across]
    planes = chain(cut, [chunks, beside, across, opposite], early, probe, cosine, sine, observed, tables)

    came = [shifted(plane, 1) for plane in planes]
    gradient, *runs = place_own(offsets, came_offsets, planes, columns)
    for c in range(2):
        gradient = add_came(came_offsets, came[c], runs[c], gradient, c)
    return gradient


def solution(mesh):
    placed = (P("cuts", None, "tile", None), P(), P(), P("tile"), P("tile"), P("tile", None, None))
    return jax.shard_map(
        per_device,
        mesh=mesh,
        in_specs=placed,
        out_specs=P("cuts", None, "tile", None),
        check_vma=False,
    )
```

```python
import jax
import jax.numpy as jnp
import numpy as np
from jax import lax
from jax.experimental import pallas as pl
from jax.experimental.pallas import tpu as pltpu
from jax.sharding import PartitionSpec as P

f32, bf16 = jnp.float32, jnp.bfloat16
LANE = 128
VMEM = pl.BlockSpec(memory_space=pltpu.VMEM)
SMEM = pl.BlockSpec(memory_space=pltpu.SMEM)
ANY = pl.BlockSpec(memory_space=pl.ANY)
SHORT = pl.CostEstimate(flops=1 << 16, bytes_accessed=1 << 12, transcendentals=0)
PARAMS = pltpu.CompilerParams(vmem_limit_bytes=12 << 20)


def dft_tables(n):
    def real_form(radix, first):
        k = np.arange(n // radix)[:, None]
        m = np.arange(n // radix)[None, :]
        angle = -2 * np.pi * ((k * (radix * m + first)) % n) / n
        c, s = np.cos(angle) / np.sqrt(n), np.sin(angle) / np.sqrt(n)
        return np.block([[c, s], [-s, c]])

    def parts(matrix):
        high = matrix.astype(np.float32).astype(jnp.bfloat16)
        low = (matrix - high.astype(np.float64)).astype(np.float32).astype(jnp.bfloat16)
        return high, low

    def for_right(matrix):
        high, low = parts(matrix)
        return np.concatenate([high, high, low], axis=0)

    def for_left(matrix):
        high, low = parts(matrix)
        return np.block([[high, high], [low, np.zeros_like(low)]])

    halves = [real_form(2, first) for first in range(2)]
    quarters = [real_form(4, first) for first in range(4)]
    right = np.stack([for_right(m) for m in halves + [m.T for m in halves]])
    left = np.stack([for_left(m) for m in [m.T for m in quarters] + quarters])
    return right, left


def pinned(x):
    return pltpu.with_memory_space_constraint(x, pltpu.HBM)


def split(x):
    high = x.astype(bf16)
    return high, (x - high.astype(f32)).astype(bf16)


def right_dot(x, table):
    high, low = split(x)
    return jnp.dot(jnp.concatenate([high, low, high], 1), table, preferred_element_type=f32)


def left_dot(table, x):
    both = jnp.dot(table, jnp.concatenate(split(x), 0), preferred_element_type=f32)
    h = both.shape[0] // 2
    return both[:h] + both[h:]


def columns_of(re, im):
    h = re.shape[1] // 2
    return (
        jnp.concatenate([re[:, :h], im[:, :h]], 1),
        jnp.concatenate([re[:, h:], im[:, h:]], 1),
    )


def planes_of(a, b):
    h = a.shape[1] // 2
    return (
        jnp.concatenate([a[:, :h], b[:, :h]], 1),
        jnp.concatenate([a[:, h:], b[:, h:]], 1),
    )


def forward(re, im, tables):
    right, left = tables
    a, b = columns_of(re, im)
    re, im = planes_of(right_dot(a + b, right[0]), right_dot(a - b, right[1]))
    q = re.shape[0] // 4
    (r0, r1, r2, r3), (i0, i1, i2, i3) = [[x[j * q : (j + 1) * q] for j in range(4)] for x in (re, im)]
    pr, pi, ur, ui = r0 + r2, i0 + i2, r0 - r2, i0 - i2
    qr, qi, vr, vi = r1 + r3, i1 + i3, r1 - r3, i1 - i3
    mixed = ((pr + qr, pi + qi), (ur + vi, ui - vr), (pr - qr, pi - qi), (ur - vi, ui + vr))
    return [left_dot(left[j], jnp.concatenate(x, 0)) for j, x in enumerate(mixed)]


def inverse(spectrum, tables):
    right, left = tables
    q = spectrum[0].shape[0] // 2
    parts = [left_dot(left[4 + j], x) for j, x in enumerate(spectrum)]
    (r0, i0), (r1, i1), (r2, i2), (r3, i3) = [(x[:q], x[q:]) for x in parts]
    ar, ai, br, bi = r0 + r2, i0 + i2, r0 - r2, i0 - i2
    cr, ci, dr, di = r1 + r3, i1 + i3, r1 - r3, i1 - i3
    re = jnp.concatenate([ar + cr, br - di, ar - cr, br + di], 0)
    im = jnp.concatenate([ai + ci, bi + dr, ai - ci, bi - dr], 0)
    a, b = columns_of(re, im)
    p, q = right_dot(a, right[2]), right_dot(b, right[3])
    return planes_of(p + q, p - q)


def times(ar, ai, br, bi):
    return ar * br - ai * bi, ar * bi + ai * br


def conj_times(ar, ai, br, bi):
    return ar * br + ai * bi, ar * bi - ai * br


def by_phase(spectrum, cosine, sine, product=times):
    q = spectrum[0].shape[0] // 2
    out = []
    for i, x in enumerate(spectrum):
        at = slice(i * q, (i + 1) * q)
        out.append(jnp.concatenate(product(cosine[at], sine[at], x[:q], x[q:]), 0))
    return out


def by_residual(spectrum, observed):
    q = spectrum[0].shape[0] // 2
    out = []
    for i, x in enumerate(spectrum):
        re, im = x[:q], x[q:]
        residual = re * re + im * im - observed[i * q : (i + 1) * q]
        out.append(jnp.concatenate([residual * re, residual * im], 0))
    return out


def prepare(prop_phase, *patterns):
    n = prop_phase.shape[0]

    def kernel(phase, *refs):
        observed, outs, (held, sem) = refs[: len(patterns)], refs[len(patterns) : -2], refs[-2:]
        row = lax.broadcasted_iota(jnp.int32, (n, n), 0)
        column = lax.broadcasted_iota(jnp.int32, (n, n), 1)
        from_row = row % (n // 4) * 4 + row // (n // 4)
        from_column = column % (n // 2) * 2 + column // (n // 2)
        left = jnp.where(column == from_row, 1.0, 0.0).astype(bf16)
        right = jnp.where(row == from_column, 1.0, 0.0).astype(bf16)

        def reorder(x):
            for side in (0, 1):
                total = None
                for _ in range(3):
                    part = x.astype(bf16)
                    x = x - part.astype(f32)
                    pair = (left, part) if side == 0 else (part, right)
                    moved = jnp.dot(*pair, preferred_element_type=f32)
                    total = moved if total is None else total + moved
                x = total
            return x

        angle = reorder(phase[...])
        copies = [pltpu.make_async_copy(held.at[i], out, sem.at[i]) for i, out in enumerate(outs)]
        values = [lambda: jnp.cos(angle), lambda: jnp.sin(angle)] + [lambda x=x: reorder(x[0]) for x in observed]
        for i, value in enumerate(values):
            held[i] = value()
            copies[i].start()
        for copy in copies:
            copy.wait()

    count = 2 + len(patterns)
    return pl.pallas_call(
        kernel,
        out_shape=[pltpu.HBM((n, n), f32)] * count,
        in_specs=[VMEM] * (1 + len(patterns)),
        out_specs=[ANY] * count,
        scratch_shapes=[pltpu.VMEM((count, n, n), f32), pltpu.SemaphoreType.DMA((count,))],
        compiler_params=PARAMS,
        cost_estimate=pl.CostEstimate(flops=36 * n**3, bytes_accessed=30 * n * n, transcendentals=2 * n * n),
    )(prop_phase, *patterns)


def run_forward(s, before, patch, after, cosine, sine, tables, ready=None):
    re, im = times(before[0], before[1], patch[0], patch[1])
    spectrum = forward(re, im, tables)
    if ready is not None:
        ready()
    spectrum = by_phase(spectrum, cosine[...], sine[...])
    re, im = inverse(spectrum, tables)
    after[0] = re
    after[1] = im


def start_chunks(sources, patch, slot, sem):
    top = 0
    for source in sources:
        rows = source.shape[1]
        pltpu.make_async_copy(source, patch.at[slot, :, pl.ds(top, rows), :], sem).start()
        top += rows


def wait_slot(patch, slot, sem):
    pltpu.make_async_copy(patch.at[slot], patch.at[slot], sem).wait()


def fetch_patches(me, sources, patch, sems, which):
    for i in which:
        start_chunks(sources[i], patch, me ^ i, sems.at[me ^ i])


def grouped(refs, patches, chunks):
    return [refs[i * chunks : (i + 1) * chunks] for i in range(patches)], refs[patches * chunks :]


def early_wave(cut, s, patches, before, cosine, sine, tables):
    n = before.shape[1]
    chunks = len(patches[0])

    def kernel(cut_ref, *refs):
        sources, rest = grouped(refs, 2, chunks)
        before, cosine, sine, right, left, wave, patch, first, phase, sem, first_sem = rest
        me = cut_ref[0]
        pairs = ((before, first), (cosine, phase.at[0]), (sine, phase.at[1]))
        copies = [pltpu.make_async_copy(x, y, first_sem.at[i]) for i, (x, y) in enumerate(pairs)]

        for i in range(2):

            @pl.when(me == s ^ i)
            def _(i=i):
                start_chunks(sources[i], patch, 0, sem)

        @pl.when(me < 2)
        def _():
            for copy in copies:
                copy.start()
            wait_slot(patch, 0, sem)
            copies[0].wait()

            def ready():
                copies[1].wait()
                copies[2].wait()

            run_forward(s, first, patch.at[0], wave, phase.at[0], phase.at[1], (right, left), ready)

    return pl.pallas_call(
        kernel,
        out_shape=jax.ShapeDtypeStruct((2, n, n), f32),
        in_specs=[SMEM] + [ANY] * (2 * chunks + 3) + [VMEM] * 2,
        out_specs=VMEM,
        scratch_shapes=[
            pltpu.VMEM((1, 2, n, n), f32),
            pltpu.VMEM((2, n, n), f32),
            pltpu.VMEM((2, n, n), f32),
            pltpu.SemaphoreType.DMA,
            pltpu.SemaphoreType.DMA((3,)),
        ],
        compiler_params=PARAMS,
        cost_estimate=SHORT,
    )(cut, *flatten(patches[:2]), before, *map(pinned, (cosine, sine)), *tables)


def flatten(patches):
    return [chunk for patch in patches for chunk in patch]


def chain(cut, patches, early, probe, cosine, sine, observed, tables):
    n = probe.shape[1]
    sections = len(patches)
    chunks = len(patches[0])
    planes_in = [cosine, sine, observed, probe, *early]

    def kernel(cut_ref, *refs):
        sources, rest = grouped(refs, sections, chunks)
        *planes, right, left, out_re, out_im, patch, waves, held, probe, sems, early_sem, held_sem = rest
        me = cut_ref[0]
        tables = (right, left)
        targets = [held.at[0], held.at[1], held.at[2], probe]
        copies = [pltpu.make_async_copy(x, y, held_sem.at[i]) for i, (x, y) in enumerate(zip(planes, targets))]
        cosine, sine, observed = [held.at[i] for i in range(3)]

        def wave(s):
            return probe if s == 0 else waves.at[s - 1]

        def back(s, re, im):
            @pl.when(me == s)
            def _():
                out_re[...], out_im[...] = conj_times(wave(s)[0], wave(s)[1], re, im)

            if s > 0:

                @pl.when(me < s)
                def _():
                    gr, gi = conj_times(patch[s, 0], patch[s, 1], re, im)
                    spectrum = by_phase(forward(gr, gi, tables), cosine[...], sine[...], conj_times)
                    back(s - 1, *inverse(spectrum, tables))

        early_copies = [pltpu.make_async_copy(planes[4 + s], waves.at[s], early_sem.at[s]) for s in range(2)]
        for odd in range(2):

            @pl.when(me % 2 == odd)
            def _(odd=odd):
                fetch_patches(me, sources, patch, sems, (2 + odd,))

        @pl.when(me < 2)
        def _():
            early_copies[1].start()

        for i in (3, 0, 1, 2):
            copies[i].start()
        for odd in range(2):

            @pl.when(me % 2 == odd)
            def _(odd=odd):
                fetch_patches(me, sources, patch, sems, (3 - odd,))

        fetch_patches(me, sources, patch, sems, (0, 1))

        def wait_phase():
            for copy in copies[:2]:
                copy.wait()

        @pl.when(me < 2)
        def _():
            early_copies[0].start()
            early_copies[1].wait()

        @pl.when(me >= 2)
        def _():
            copies[3].wait()
            for s in range(2):
                wait_slot(patch, s, sems.at[s])
                ready = wait_phase if s == 0 else None
                run_forward(s, wave(s), patch.at[s], waves.at[s], cosine, sine, tables, ready)

        for s in range(2, sections):
            wait_slot(patch, s, sems.at[s])
            if s < sections - 1:
                ready = (lambda: pl.when(me < 2)(wait_phase)) if s == 2 else None
                run_forward(s, wave(s), patch.at[s], waves.at[s], cosine, sine, tables, ready)
        copies[2].wait()

        @pl.when(me < 2)
        def _():
            copies[3].wait()
            early_copies[0].wait()
            for s in range(2):
                wait_slot(patch, s, sems.at[s])

        last = sections - 1
        re, im = times(wave(last)[0], wave(last)[1], patch[last, 0], patch[last, 1])
        spectrum = by_residual(forward(re, im, tables), observed[...])
        back(last, *inverse(spectrum, tables))

    return pl.pallas_call(
        kernel,
        out_shape=[jax.ShapeDtypeStruct((n, n), f32)] * 2,
        in_specs=[SMEM] + [ANY] * (sections * chunks + len(planes_in)) + [VMEM] * 2,
        out_specs=[VMEM] * 2,
        scratch_shapes=[
            pltpu.VMEM((sections, 2, n, n), f32),
            pltpu.VMEM((sections - 1, 2, n, n), f32),
            pltpu.VMEM((3, n, n), f32),
            pltpu.VMEM((2, n, n), f32),
            pltpu.SemaphoreType.DMA((sections,)),
            pltpu.SemaphoreType.DMA((2,)),
            pltpu.SemaphoreType.DMA((4,)),
        ],
        compiler_params=PARAMS,
        cost_estimate=pl.CostEstimate(flops=10 * 24 * n**3, bytes_accessed=16 * n * n, transcendentals=0),
    )(cut, *flatten(patches), *map(pinned, (cosine, sine, observed, probe)), *early, *tables)


def window_start(column, width, columns):
    start = jnp.minimum(column // LANE * LANE, columns - width - LANE)
    return pl.multiple_of(start, LANE), column - start


def staged(strip):
    def kernel(strip, out, sem):
        copy = pltpu.make_async_copy(strip, out, sem)
        copy.start()
        copy.wait()

    return pl.pallas_call(
        kernel,
        out_shape=pltpu.VMEM(strip.shape, f32),
        in_specs=[ANY],
        out_specs=VMEM,
        scratch_shapes=[pltpu.SemaphoreType.DMA],
        compiler_params=PARAMS,
    )(pinned(strip))


def cut_window(offsets, strip, width, bounds):
    _, _, rows, columns = strip.shape
    chunks = len(bounds) - 1

    def kernel(offsets, strip, *outs):
        row, column = offsets[0], offsets[1]
        start, shift = window_start(column, width, columns)
        for c in range(2):
            x = strip[0, c, :, pl.ds(start, width + LANE)]
            x = pltpu.roll(x, lax.rem(width + LANE - shift, width + LANE), 1)[:, :width]
            x = pltpu.roll(x, lax.rem(rows - row, rows), 0)
            for j in range(chunks):
                outs[j][c] = x[bounds[j] : bounds[j + 1]]

    return pl.pallas_call(
        kernel,
        out_shape=[jax.ShapeDtypeStruct((2, bounds[j + 1] - bounds[j], width), f32) for j in range(chunks)],
        in_specs=[SMEM, VMEM],
        out_specs=[VMEM] * chunks,
        compiler_params=PARAMS,
    )(offsets, strip)


def moved(piece, row, shift, keep):
    return shifted_right(jnp.where(keep, pltpu.roll(piece, row, 0), 0.0), shift)


def shifted_right(x, shift):
    return pltpu.roll(jnp.concatenate([x, jnp.zeros((x.shape[0], LANE), f32)], 1), shift, 1)


def place_own(offsets, came_offsets, planes, columns):
    rows, width = planes[0].shape

    def kernel(offsets, came_offsets, re, im, out, *runs):
        index = lax.broadcasted_iota(jnp.int32, (rows, width), 0)
        out[...] = jnp.zeros_like(out)
        row = offsets[0]
        start, shift = window_start(offsets[1], width, columns)
        came_start, _ = window_start(came_offsets[1], width, columns)
        for c, plane in enumerate((re, im)):
            out[0, c, :, pl.ds(start, width + LANE)] = moved(plane[...], row, shift, index >= row)
            runs[c][...] = out[0, c, :, pl.ds(came_start, width + LANE)]

    return pl.pallas_call(
        kernel,
        out_shape=[jax.ShapeDtypeStruct((1, 2, rows, columns), f32)] + [pltpu.VMEM((rows, width + LANE), f32)] * 2,
        in_specs=[SMEM, SMEM, VMEM, VMEM],
        out_specs=[VMEM] * 3,
        compiler_params=PARAMS,
    )(offsets, came_offsets, *planes)


def add_came(offsets, came, run, base, c):
    rows, width = came.shape
    columns = base.shape[3]

    parts = 4
    step = rows // parts

    def kernel(offsets, came, run, base, out, wide, sem):
        row = offsets[0]
        start, shift = window_start(offsets[1], width, columns)
        index = lax.broadcasted_iota(jnp.int32, (rows, width), 0)
        x = jnp.where(index < row, pltpu.roll(came[...], row, 0), 0.0)
        writes = []
        for part in range(parts):
            at = pl.ds(part * step, step)
            wide[at] = run[at] + shifted_right(x[part * step : (part + 1) * step], shift)
            to = out.at[0, c, at, pl.ds(start, width + LANE)]
            writes.append(pltpu.make_async_copy(wide.at[at], to, sem.at[part]))
            writes[-1].start()
        for write in writes:
            write.wait()

    return pl.pallas_call(
        kernel,
        out_shape=jax.ShapeDtypeStruct(base.shape, f32),
        in_specs=[SMEM, VMEM, VMEM, ANY],
        out_specs=ANY,
        input_output_aliases={3: 0},
        scratch_shapes=[pltpu.VMEM((rows, width + LANE), f32), pltpu.SemaphoreType.DMA((parts,))],
        compiler_params=PARAMS,
    )(offsets, came, run, pinned(base))


def shifted(value, by):
    devices = lax.axis_size("tile")
    pairs = [(i, i + by) for i in range(devices) if 0 <= i + by < devices]
    return lax.ppermute(value, "tile", pairs)


def swapped(value, bit):
    devices = lax.axis_size("cuts")
    return lax.ppermute(value, "cuts", [(i, i ^ bit) for i in range(devices)])


def after(*values):
    return lax.optimization_barrier(values)


def merged(first, second, top, row, rows):
    index = lax.broadcasted_iota(jnp.int32, first.shape, 1) + top
    return jnp.where(index < rows - row, first, second)


BOUNDS = (0, 152, 256)


def per_device(transmission, probe, prop_phase, row_off, col_off, measured):
    rows, columns = transmission.shape[2:]
    width = probe.shape[1]
    cut = lax.axis_index("cuts").astype(jnp.int32).reshape(1)
    offsets = jnp.concatenate([row_off, col_off])
    strip = staged(transmission)
    came_offsets = shifted(offsets, 1)
    cosine, sine, observed = prepare(prop_phase, measured)
    bands = list(cut_window(came_offsets, strip, width, BOUNDS))
    below = [shifted(band, -1) for band in bands]
    own = cut_window(offsets, strip, width, BOUNDS)
    tables = [jnp.asarray(t) for t in dft_tables(width)]

    chunks, across = [], []
    below[0], cosine, sine, observed = after(below[0], cosine, sine, observed)
    for j, (first, second) in enumerate(zip(own, below)):
        if chunks:
            first, second, chunks[-1] = after(first, second, chunks[-1])
        chunks.append(merged(first, second, BOUNDS[j], row_off[0], rows))
        chunk = chunks[-1]
        across.append(swapped(chunk, 2))
    beside = [swapped(chunk, 1) for chunk in chunks]
    early = [early_wave(cut, 0, [chunks, beside], pinned(probe), cosine, sine, tables)]
    across[0], early[0] = after(across[0], early[0])
    early.append(early_wave(cut, 1, [chunks, beside], early[0], cosine, sine, tables))
    across[1], early[1] = after(across[1], early[1])
    opposite = [swapped(chunk, 1) for chunk in across]
    planes = chain(cut, [chunks, beside, across, opposite], early, probe, cosine, sine, observed, tables)

    came = [shifted(plane, 1) for plane in planes]
    gradient, *runs = place_own(offsets, came_offsets, planes, columns)
    for c in range(2):
        gradient = add_came(came_offsets, came[c], runs[c], gradient, c)
    return gradient


def solution(mesh):
    placed = (P("cuts", None, "tile", None), P(), P(), P("tile"), P("tile"), P("tile", None, None))
    return jax.shard_map(
        per_device,
        mesh=mesh,
        in_specs=placed,
        out_specs=P("cuts", None, "tile", None),
        check_vma=False,
    )
```

```python
import jax
import jax.numpy as jnp
import numpy as np
from jax import lax
from jax.experimental import pallas as pl
from jax.experimental.pallas import tpu as pltpu
from jax.sharding import PartitionSpec as P

f32, bf16 = jnp.float32, jnp.bfloat16
LANE = 128
VMEM = pl.BlockSpec(memory_space=pltpu.VMEM)
SMEM = pl.BlockSpec(memory_space=pltpu.SMEM)
ANY = pl.BlockSpec(memory_space=pl.ANY)
SHORT = pl.CostEstimate(flops=1 << 16, bytes_accessed=1 << 12, transcendentals=0)
PARAMS = pltpu.CompilerParams(vmem_limit_bytes=12 << 20)


def dft_tables(n):
    def real_form(radix, first):
        k = np.arange(n // radix)[:, None]
        m = np.arange(n // radix)[None, :]
        angle = -2 * np.pi * ((k * (radix * m + first)) % n) / n
        c, s = np.cos(angle) / np.sqrt(n), np.sin(angle) / np.sqrt(n)
        return np.block([[c, s], [-s, c]])

    def parts(matrix):
        high = matrix.astype(np.float32).astype(jnp.bfloat16)
        low = (matrix - high.astype(np.float64)).astype(np.float32).astype(jnp.bfloat16)
        return high, low

    def for_right(matrix):
        high, low = parts(matrix)
        return np.concatenate([high, high, low], axis=0)

    def for_left(matrix):
        high, low = parts(matrix)
        return np.block([[high, high], [low, np.zeros_like(low)]])

    halves = [real_form(2, first) for first in range(2)]
    quarters = [real_form(4, first) for first in range(4)]
    right = np.stack([for_right(m) for m in halves + [m.T for m in halves]])
    left = np.stack([for_left(m) for m in [m.T for m in quarters] + quarters])
    return right, left


def pinned(x):
    return pltpu.with_memory_space_constraint(x, pltpu.HBM)


def split(x):
    high = x.astype(bf16)
    return high, (x - high.astype(f32)).astype(bf16)


def right_dot(x, table):
    high, low = split(x)
    return jnp.dot(jnp.concatenate([high, low, high], 1), table, preferred_element_type=f32)


def left_dot(table, x):
    both = jnp.dot(table, jnp.concatenate(split(x), 0), preferred_element_type=f32)
    h = both.shape[0] // 2
    return both[:h] + both[h:]


def columns_of(re, im):
    h = re.shape[1] // 2
    return (
        jnp.concatenate([re[:, :h], im[:, :h]], 1),
        jnp.concatenate([re[:, h:], im[:, h:]], 1),
    )


def planes_of(a, b):
    h = a.shape[1] // 2
    return (
        jnp.concatenate([a[:, :h], b[:, :h]], 1),
        jnp.concatenate([a[:, h:], b[:, h:]], 1),
    )


def forward(re, im, tables):
    right, left = tables
    a, b = columns_of(re, im)
    re, im = planes_of(right_dot(a + b, right[0]), right_dot(a - b, right[1]))
    q = re.shape[0] // 4
    (r0, r1, r2, r3), (i0, i1, i2, i3) = [[x[j * q : (j + 1) * q] for j in range(4)] for x in (re, im)]
    pr, pi, ur, ui = r0 + r2, i0 + i2, r0 - r2, i0 - i2
    qr, qi, vr, vi = r1 + r3, i1 + i3, r1 - r3, i1 - i3
    mixed = ((pr + qr, pi + qi), (ur + vi, ui - vr), (pr - qr, pi - qi), (ur - vi, ui + vr))
    return [left_dot(left[j], jnp.concatenate(x, 0)) for j, x in enumerate(mixed)]


def inverse(spectrum, tables):
    right, left = tables
    q = spectrum[0].shape[0] // 2
    parts = [left_dot(left[4 + j], x) for j, x in enumerate(spectrum)]
    (r0, i0), (r1, i1), (r2, i2), (r3, i3) = [(x[:q], x[q:]) for x in parts]
    ar, ai, br, bi = r0 + r2, i0 + i2, r0 - r2, i0 - i2
    cr, ci, dr, di = r1 + r3, i1 + i3, r1 - r3, i1 - i3
    re = jnp.concatenate([ar + cr, br - di, ar - cr, br + di], 0)
    im = jnp.concatenate([ai + ci, bi + dr, ai - ci, bi - dr], 0)
    a, b = columns_of(re, im)
    p, q = right_dot(a, right[2]), right_dot(b, right[3])
    return planes_of(p + q, p - q)


def times(ar, ai, br, bi):
    return ar * br - ai * bi, ar * bi + ai * br


def conj_times(ar, ai, br, bi):
    return ar * br + ai * bi, ar * bi - ai * br


def by_phase(spectrum, cosine, sine, product=times):
    q = spectrum[0].shape[0] // 2
    out = []
    for i, x in enumerate(spectrum):
        at = slice(i * q, (i + 1) * q)
        out.append(jnp.concatenate(product(cosine[at], sine[at], x[:q], x[q:]), 0))
    return out


def by_residual(spectrum, observed):
    q = spectrum[0].shape[0] // 2
    out = []
    for i, x in enumerate(spectrum):
        re, im = x[:q], x[q:]
        residual = re * re + im * im - observed[i * q : (i + 1) * q]
        out.append(jnp.concatenate([residual * re, residual * im], 0))
    return out


def prepare(prop_phase, *patterns):
    n = prop_phase.shape[0]

    def kernel(phase, *refs):
        observed, outs, (held, sem) = refs[: len(patterns)], refs[len(patterns) : -2], refs[-2:]
        row = lax.broadcasted_iota(jnp.int32, (n, n), 0)
        column = lax.broadcasted_iota(jnp.int32, (n, n), 1)
        from_row = row % (n // 4) * 4 + row // (n // 4)
        from_column = column % (n // 2) * 2 + column // (n // 2)
        left = jnp.where(column == from_row, 1.0, 0.0).astype(bf16)
        right = jnp.where(row == from_column, 1.0, 0.0).astype(bf16)

        def reorder(x):
            for side in (0, 1):
                total = None
                for _ in range(3):
                    part = x.astype(bf16)
                    x = x - part.astype(f32)
                    pair = (left, part) if side == 0 else (part, right)
                    moved = jnp.dot(*pair, preferred_element_type=f32)
                    total = moved if total is None else total + moved
                x = total
            return x

        angle = reorder(phase[...])
        copies = [pltpu.make_async_copy(held.at[i], out, sem.at[i]) for i, out in enumerate(outs)]
        values = [lambda: jnp.cos(angle), lambda: jnp.sin(angle)] + [lambda x=x: reorder(x[0]) for x in observed]
        for i, value in enumerate(values):
            held[i] = value()
            copies[i].start()
        for copy in copies:
            copy.wait()

    count = 2 + len(patterns)
    return pl.pallas_call(
        kernel,
        out_shape=[pltpu.HBM((n, n), f32)] * count,
        in_specs=[VMEM] * (1 + len(patterns)),
        out_specs=[ANY] * count,
        scratch_shapes=[pltpu.VMEM((count, n, n), f32), pltpu.SemaphoreType.DMA((count,))],
        compiler_params=PARAMS,
        cost_estimate=pl.CostEstimate(flops=36 * n**3, bytes_accessed=30 * n * n, transcendentals=2 * n * n),
    )(prop_phase, *patterns)


def run_forward(s, before, patch, after, cosine, sine, tables, ready=None):
    re, im = times(before[0], before[1], patch[0], patch[1])
    spectrum = forward(re, im, tables)
    if ready is not None:
        ready()
    spectrum = by_phase(spectrum, cosine[...], sine[...])
    re, im = inverse(spectrum, tables)
    after[0] = re
    after[1] = im


def start_chunks(sources, patch, slot, sem):
    top = 0
    for source in sources:
        rows = source.shape[1]
        pltpu.make_async_copy(source, patch.at[slot, :, pl.ds(top, rows), :], sem).start()
        top += rows


def wait_slot(patch, slot, sem):
    pltpu.make_async_copy(patch.at[slot], patch.at[slot], sem).wait()


def fetch_patches(me, sources, patch, sems, which):
    for i in which:
        start_chunks(sources[i], patch, me ^ i, sems.at[me ^ i])


def grouped(refs, patches, chunks):
    return [refs[i * chunks : (i + 1) * chunks] for i in range(patches)], refs[patches * chunks :]


def early_waves(cut, patches, probe, cosine, sine, tables):
    n = probe.shape[1]
    chunks = len(patches[0])

    def kernel(cut_ref, *refs):
        sources, rest = grouped(refs, 2, chunks)
        probe, cosine, sine, right, left, waves, patch, first, phase, sems, phase_sem = rest
        me = cut_ref[0]
        pairs = ((probe, first), (cosine, phase.at[0]), (sine, phase.at[1]))
        copies = [pltpu.make_async_copy(x, y, phase_sem.at[i]) for i, (x, y) in enumerate(pairs)]

        @pl.when(me < 2)
        def _():
            fetch_patches(me, sources, patch, sems, (0, 1))
            for copy in copies:
                copy.start()
            before = first
            for s in range(2):
                wait_slot(patch, s, sems.at[s])
                if s == 0:
                    for copy in copies:
                        copy.wait()
                run_forward(s, before, patch.at[s], waves.at[s], phase.at[0], phase.at[1], (right, left))
                before = waves.at[s]

    return pl.pallas_call(
        kernel,
        out_shape=jax.ShapeDtypeStruct((2, 2, n, n), f32),
        in_specs=[SMEM] + [ANY] * (2 * chunks + 3) + [VMEM] * 2,
        out_specs=VMEM,
        scratch_shapes=[
            pltpu.VMEM((2, 2, n, n), f32),
            pltpu.VMEM((2, n, n), f32),
            pltpu.VMEM((2, n, n), f32),
            pltpu.SemaphoreType.DMA((2,)),
            pltpu.SemaphoreType.DMA((3,)),
        ],
        compiler_params=PARAMS,
        cost_estimate=SHORT,
    )(cut, *flatten(patches[:2]), *map(pinned, (probe, cosine, sine)), *tables)


def flatten(patches):
    return [chunk for patch in patches for chunk in patch]


def chain(cut, patches, early, probe, cosine, sine, observed, tables):
    n = probe.shape[1]
    sections = len(patches)
    chunks = len(patches[0])
    planes_in = [cosine, sine, observed, probe, early]

    def kernel(cut_ref, *refs):
        sources, rest = grouped(refs, sections, chunks)
        *planes, right, left, out_re, out_im, patch, waves, held, probe, sems, early_sem, held_sem = rest
        me = cut_ref[0]
        tables = (right, left)
        targets = [held.at[0], held.at[1], held.at[2], probe]
        copies = [pltpu.make_async_copy(x, y, held_sem.at[i]) for i, (x, y) in enumerate(zip(planes, targets))]
        cosine, sine, observed = [held.at[i] for i in range(3)]

        def wave(s):
            return probe if s == 0 else waves.at[s - 1]

        def back(s, re, im):
            @pl.when(me == s)
            def _():
                out_re[...], out_im[...] = conj_times(wave(s)[0], wave(s)[1], re, im)

            if s > 0:

                @pl.when(me < s)
                def _():
                    gr, gi = conj_times(patch[s, 0], patch[s, 1], re, im)
                    spectrum = by_phase(forward(gr, gi, tables), cosine[...], sine[...], conj_times)
                    back(s - 1, *inverse(spectrum, tables))

        early_copies = [pltpu.make_async_copy(planes[4].at[s], waves.at[s], early_sem.at[s]) for s in range(2)]
        for odd in range(2):

            @pl.when(me % 2 == odd)
            def _(odd=odd):
                fetch_patches(me, sources, patch, sems, (2 + odd,))

        @pl.when(me < 2)
        def _():
            early_copies[1].start()

        for i in (3, 0, 1, 2):
            copies[i].start()
        for odd in range(2):

            @pl.when(me % 2 == odd)
            def _(odd=odd):
                fetch_patches(me, sources, patch, sems, (3 - odd,))

        fetch_patches(me, sources, patch, sems, (0, 1))

        def wait_phase():
            for copy in copies[:2]:
                copy.wait()

        @pl.when(me < 2)
        def _():
            early_copies[0].start()
            early_copies[1].wait()

        @pl.when(me >= 2)
        def _():
            copies[3].wait()
            for s in range(2):
                wait_slot(patch, s, sems.at[s])
                ready = wait_phase if s == 0 else None
                run_forward(s, wave(s), patch.at[s], waves.at[s], cosine, sine, tables, ready)

        for s in range(2, sections):
            wait_slot(patch, s, sems.at[s])
            if s < sections - 1:
                ready = (lambda: pl.when(me < 2)(wait_phase)) if s == 2 else None
                run_forward(s, wave(s), patch.at[s], waves.at[s], cosine, sine, tables, ready)
        copies[2].wait()

        @pl.when(me < 2)
        def _():
            copies[3].wait()
            early_copies[0].wait()
            for s in range(2):
                wait_slot(patch, s, sems.at[s])

        last = sections - 1
        re, im = times(wave(last)[0], wave(last)[1], patch[last, 0], patch[last, 1])
        spectrum = by_residual(forward(re, im, tables), observed[...])
        back(last, *inverse(spectrum, tables))

    return pl.pallas_call(
        kernel,
        out_shape=[jax.ShapeDtypeStruct((n, n), f32)] * 2,
        in_specs=[SMEM] + [ANY] * (sections * chunks + len(planes_in)) + [VMEM] * 2,
        out_specs=[VMEM] * 2,
        scratch_shapes=[
            pltpu.VMEM((sections, 2, n, n), f32),
            pltpu.VMEM((sections - 1, 2, n, n), f32),
            pltpu.VMEM((3, n, n), f32),
            pltpu.VMEM((2, n, n), f32),
            pltpu.SemaphoreType.DMA((sections,)),
            pltpu.SemaphoreType.DMA((2,)),
            pltpu.SemaphoreType.DMA((4,)),
        ],
        compiler_params=PARAMS,
        cost_estimate=pl.CostEstimate(flops=10 * 24 * n**3, bytes_accessed=16 * n * n, transcendentals=0),
    )(cut, *flatten(patches), *map(pinned, (cosine, sine, observed, probe)), early, *tables)


def window_start(column, width, columns):
    start = jnp.minimum(column // LANE * LANE, columns - width - LANE)
    return pl.multiple_of(start, LANE), column - start


def staged(strip):
    def kernel(strip, out, sem):
        copy = pltpu.make_async_copy(strip, out, sem)
        copy.start()
        copy.wait()

    return pl.pallas_call(
        kernel,
        out_shape=pltpu.VMEM(strip.shape, f32),
        in_specs=[ANY],
        out_specs=VMEM,
        scratch_shapes=[pltpu.SemaphoreType.DMA],
        compiler_params=PARAMS,
    )(pinned(strip))


def cut_window(offsets, strip, width, bounds):
    _, _, rows, columns = strip.shape
    chunks = len(bounds) - 1

    def kernel(offsets, strip, *outs):
        row, column = offsets[0], offsets[1]
        start, shift = window_start(column, width, columns)
        for c in range(2):
            x = strip[0, c, :, pl.ds(start, width + LANE)]
            x = pltpu.roll(x, lax.rem(width + LANE - shift, width + LANE), 1)[:, :width]
            x = pltpu.roll(x, lax.rem(rows - row, rows), 0)
            for j in range(chunks):
                outs[j][c] = x[bounds[j] : bounds[j + 1]]

    return pl.pallas_call(
        kernel,
        out_shape=[jax.ShapeDtypeStruct((2, bounds[j + 1] - bounds[j], width), f32) for j in range(chunks)],
        in_specs=[SMEM, VMEM],
        out_specs=[VMEM] * chunks,
        compiler_params=PARAMS,
    )(offsets, strip)


def moved(piece, row, shift, keep):
    return shifted_right(jnp.where(keep, pltpu.roll(piece, row, 0), 0.0), shift)


def shifted_right(x, shift):
    return pltpu.roll(jnp.concatenate([x, jnp.zeros((x.shape[0], LANE), f32)], 1), shift, 1)


def place_own(offsets, came_offsets, planes, columns):
    rows, width = planes[0].shape

    def kernel(offsets, came_offsets, re, im, out, *runs):
        index = lax.broadcasted_iota(jnp.int32, (rows, width), 0)
        out[...] = jnp.zeros_like(out)
        row = offsets[0]
        start, shift = window_start(offsets[1], width, columns)
        came_start, _ = window_start(came_offsets[1], width, columns)
        for c, plane in enumerate((re, im)):
            out[0, c, :, pl.ds(start, width + LANE)] = moved(plane[...], row, shift, index >= row)
            runs[c][...] = out[0, c, :, pl.ds(came_start, width + LANE)]

    return pl.pallas_call(
        kernel,
        out_shape=[jax.ShapeDtypeStruct((1, 2, rows, columns), f32)] + [pltpu.VMEM((rows, width + LANE), f32)] * 2,
        in_specs=[SMEM, SMEM, VMEM, VMEM],
        out_specs=[VMEM] * 3,
        compiler_params=PARAMS,
    )(offsets, came_offsets, *planes)


def add_came(offsets, came, run, base, c):
    rows, width = came.shape
    columns = base.shape[3]

    parts = 8
    step = rows // parts

    def kernel(offsets, came, run, base, out, wide, sem):
        row = offsets[0]
        start, shift = window_start(offsets[1], width, columns)
        index = lax.broadcasted_iota(jnp.int32, (rows, width), 0)
        x = jnp.where(index < row, pltpu.roll(came[...], row, 0), 0.0)
        writes = []
        for part in range(parts):
            at = pl.ds(part * step, step)
            wide[at] = run[at] + shifted_right(x[part * step : (part + 1) * step], shift)
            to = out.at[0, c, at, pl.ds(start, width + LANE)]
            writes.append(pltpu.make_async_copy(wide.at[at], to, sem.at[part]))
            writes[-1].start()
        for write in writes:
            write.wait()

    return pl.pallas_call(
        kernel,
        out_shape=jax.ShapeDtypeStruct(base.shape, f32),
        in_specs=[SMEM, VMEM, VMEM, ANY],
        out_specs=ANY,
        input_output_aliases={3: 0},
        scratch_shapes=[pltpu.VMEM((rows, width + LANE), f32), pltpu.SemaphoreType.DMA((parts,))],
        compiler_params=PARAMS,
    )(offsets, came, run, pinned(base))


def shifted(value, by):
    devices = lax.axis_size("tile")
    pairs = [(i, i + by) for i in range(devices) if 0 <= i + by < devices]
    return lax.ppermute(value, "tile", pairs)


def swapped(value, bit):
    devices = lax.axis_size("cuts")
    return lax.ppermute(value, "cuts", [(i, i ^ bit) for i in range(devices)])


def after(*values):
    return lax.optimization_barrier(values)


def merged(first, second, top, row, rows):
    index = lax.broadcasted_iota(jnp.int32, first.shape, 1) + top
    return jnp.where(index < rows - row, first, second)


BOUNDS = (0, 152, 256)


def per_device(transmission, probe, prop_phase, row_off, col_off, measured):
    rows, columns = transmission.shape[2:]
    width = probe.shape[1]
    cut = lax.axis_index("cuts").astype(jnp.int32).reshape(1)
    offsets = jnp.concatenate([row_off, col_off])
    strip = staged(transmission)
    came_offsets = shifted(offsets, 1)
    cosine, sine, observed = prepare(prop_phase, measured)
    bands = list(cut_window(came_offsets, strip, width, BOUNDS))
    below = [shifted(band, -1) for band in bands]
    own = cut_window(offsets, strip, width, BOUNDS)
    tables = [jnp.asarray(t) for t in dft_tables(width)]

    chunks, across = [], []
    below[0], cosine, sine, observed = after(below[0], cosine, sine, observed)
    for j, (first, second) in enumerate(zip(own, below)):
        if chunks:
            first, second, chunks[-1] = after(first, second, chunks[-1])
        chunks.append(merged(first, second, BOUNDS[j], row_off[0], rows))
        chunk = chunks[-1]
        across.append(swapped(chunk, 2))
    beside = [swapped(chunk, 1) for chunk in chunks]
    across[0], beside[0] = after(across[0], beside[0])
    early = early_waves(cut, [chunks, beside], probe, cosine, sine, tables)
    across[1], early = after(across[1], early)
    opposite = [swapped(chunk, 1) for chunk in across]
    planes = chain(cut, [chunks, beside, across, opposite], early, probe, cosine, sine, observed, tables)

    came = [shifted(plane, 1) for plane in planes]
    gradient, *runs = place_own(offsets, came_offsets, planes, columns)
    for c in range(2):
        gradient = add_came(came_offsets, came[c], runs[c], gradient, c)
    return gradient


def solution(mesh):
    placed = (P("cuts", None, "tile", None), P(), P(), P("tile"), P("tile"), P("tile", None, None))
    return jax.shard_map(
        per_device,
        mesh=mesh,
        in_specs=placed,
        out_specs=P("cuts", None, "tile", None),
        check_vma=False,
    )
```
